32 devices in a mesh: wide: 4 (over y, core), node: 8 (over z, x).
Axes of the slice: x: 2, y: 2, z: 4, core: 2. Of those that a mesh axis runs over, the one named last changes fastest.
Arguments:
- tokens: bfloat16 [16384, 4096], P(('wide', 'node')), may hold values from -6 to 6
- key_weight: bfloat16 [4096, 512], P(('node', 'wide')), may hold values from -0.09375 to 0.09375
- cotangent: bfloat16 [16384, 512], P(('wide', 'node')), may hold values from -6 to 6
Outputs:
- keys: bfloat16 [16384, 512], P(('wide', 'node'))
- input_grad: bfloat16 [16384, 4096], P(('wide', 'node'))
- weight_grad: float32 [4096, 512], P(('node', 'wide'))
The draws below stay inside these ranges and needn't reach their ends.
All inputs are finite; a program needn't handle non-finite values.
Results may differ from the reference program's by a relative error of at most 0.001.
Values may be sent and summed in bfloat16 or wider, within the bound.
No kernel may reach another device: no remote copies, remote signals or barrier semaphores. Data moves between devices by JAX's collectives and lax.ppermute only.
A program may use at most 64 MiB of HBM per device.

```python
import jax
import jax.numpy as jnp
from jax import lax

D = 4096
TOK_DEV = 512
KD = 512
TOKENS = 16384


def raised(values, own_key, source, target, shards_of, factor):
    def block_of(position):
        return (jnp.arange(values.shape[position]) // (values.shape[position] // shards_of)).reshape((-1,) + (1,) * (values.ndim - 1 - position))

    near = jax.random.permutation(own_key, shards_of)[block_of(target)]
    far = (block_of(target) + shards_of // 2) % shards_of
    return jnp.where((block_of(source) == near) | (block_of(source) == far), factor * values, values)


def shard_levels(stream_key, extent, cuts, least, top_value):
    level = 1.0
    for position, parts in cuts:
        steps = jax.random.uniform(jax.random.fold_in(jax.random.fold_in(stream_key, 6), position), (parts,), jnp.float32, least / len(cuts), top_value / len(cuts))
        level = level * jnp.repeat(jnp.exp(steps), extent[position] // parts).reshape((-1,) + (1,) * (len(extent) - 1 - position))
    return level


def gaussian(own_key, dims, deviation, reach, shards=(), kind=jnp.bfloat16):
    result = jax.random.normal(own_key, dims, jnp.float32) * deviation
    if len(shards) > 0:
        result = shard_levels(own_key, dims, shards, -0.22, 0.18) * result
    return jnp.clip(result, min=-reach, max=reach).astype(kind)


def heavy_noise(own_key, extent, width, limit, shards, heavy, kind=jnp.bfloat16):
    drawn = width * jax.random.normal(own_key, extent, jnp.float32)
    if shards:
        drawn = drawn * shard_levels(own_key, extent, shards, -0.22, 0.18)
    return jnp.clip(raised(drawn, jax.random.fold_in(own_key, 3), *heavy), -limit, limit).astype(kind)


def setup_inputs(seed: int = 0) -> dict:
    splits = jax.random.split(jax.random.key(seed), 4)
    return {
        "tokens": heavy_noise(splits[0], (TOKENS, D), 1.0, 6.0, ((0, 32),), (0, 1, 32, 2.75)),
        "key_weight": gaussian(splits[1], (D, KD), D ** -0.5, 0.09375, ((0, 32),)),
        "cotangent": gaussian(splits[2], (TOKENS, KD), 1.0, 6.0, ((0, 32),)),
    }


def reference(tokens, key_weight, cotangent):
    keys = jnp.dot(tokens, key_weight, preferred_element_type=jnp.float32).astype(jnp.bfloat16)
    input_grad = jnp.dot(cotangent, key_weight.T, preferred_element_type=jnp.float32).astype(jnp.bfloat16)
    blocks = TOKENS // TOK_DEV
    tok_blocks = tokens.reshape(blocks, TOK_DEV, D)
    cot_blocks = cotangent.reshape(blocks, TOK_DEV, KD)

    def add_block(total, pair):
        part = jnp.dot(pair[0].T, pair[1], preferred_element_type=jnp.float32)
        return (total + part, None)
    total, _ = lax.scan(add_block, jnp.zeros((D, KD), jnp.float32), (tok_blocks, cot_blocks))
    weight_grad = total * (1.0 / jnp.sqrt(jnp.float32(TOKENS)))
    return (keys, input_grad, weight_grad)
```

```python
import jax
import jax.numpy as jnp
from jax import lax
from jax.sharding import PartitionSpec as P

AXES = ("wide", "node")


def on_device(tokens, key_weight, cotangent):
    wide, node = lax.axis_size("wide"), lax.axis_size("node")
    w_me, n_me = lax.axis_index("wide"), lax.axis_index("node")
    rows, kd = key_weight.shape
    half = rows // 2
    ny, nx, nz = wide // 2, 2, node // 2
    core, y_me = w_me % 2, w_me // 2
    x_me, z_me = n_me % 2, n_me // 2

    def swap(value, name, j):
        mask = {"core": j * node, "y": 2 * j * node, "x": j, "z": 2 * j}[name]
        return lax.ppermute(value, AXES, [(i, i ^ mask) for i in range(wide * node)])

    def gathered(value, name, size, me):
        parts = [value] + [swap(value, name, j) for j in range(1, size)]
        out = jnp.zeros((size,) + value.shape, value.dtype)
        for j in range(size):
            out = lax.dynamic_update_index_in_dim(out, parts[j], me ^ j, 0)
        return out

    def pick(value, axis, index):
        return lax.dynamic_index_in_dim(value, index, axis, keepdims=False)

    def summed(value, axis, name, size, me, scale):
        total = pick(value, axis, me).astype(jnp.float32)
        for j in range(1, size):
            sent = pick(value, axis, me ^ j)
            total = total + swap(sent, name, j).astype(jnp.float32)
        return total * scale

    tok_top = jnp.max(jnp.abs(tokens), axis=1).astype(jnp.float32)
    cot_top = jnp.max(jnp.abs(cotangent), axis=1).astype(jnp.float32)
    bound = jnp.full((8, 128), jnp.sum(tok_top * cot_top))
    pair = bound + swap(bound, "core", 1)
    whole = pair
    for name, size in (("x", nx), ("y", ny), ("z", nz)):
        bit = 1
        while bit < size:
            whole = whole + swap(whole, name, bit)
            bit *= 2
    pair = jnp.maximum(pair[0, 0], 1e-33)
    whole = jnp.maximum(whole[0, 0], 1e-33)

    gz = gathered(key_weight, "z", nz, z_me).reshape(nz, 2, half, kd)
    one = gathered(gathered(gz[:, 0], "x", nx, x_me), "y", ny, y_me)
    two = gathered(gathered(gz[:, 1], "y", ny, y_me), "x", nx, x_me)
    both = jnp.stack([one.transpose(2, 1, 0, 3, 4), two.transpose(2, 0, 1, 3, 4)], axis=3)
    weight = gathered(both, "core", 2, core)
    weight = weight.transpose(1, 2, 3, 0, 4, 5, 6).reshape(node * wide * rows, kd)

    part = lax.dot_general(
        tokens, cotangent, (((0,), (0,)), ((), ())), preferred_element_type=jnp.float32
    )
    part = (part * (32768.0 / pair)).astype(jnp.float16)
    part = part.reshape(nz * nx * ny, 2, rows, kd)
    part = summed(part, 1, "core", 2, core, pair / whole).astype(jnp.float16)
    part = part.reshape(nz, nx, ny, 2, half, kd)
    one = summed(part[:, :, :, 0], 1, "x", nx, x_me, 1.0).astype(jnp.float16)
    one = summed(one, 1, "y", ny, y_me, 1.0)
    two = summed(part[:, :, :, 1], 2, "y", ny, y_me, 1.0).astype(jnp.float16)
    two = summed(two, 1, "x", nx, x_me, 1.0)
    part = jnp.concatenate([one, two], axis=1).astype(jnp.float16)
    total_tokens = tokens.shape[0] * wide * node
    weight_grad = summed(
        part, 0, "z", nz, z_me, (whole / 32768.0) * (1.0 / jnp.sqrt(jnp.float32(total_tokens)))
    )

    keys = jnp.dot(tokens, weight, preferred_element_type=jnp.float32).astype(jnp.bfloat16)
    input_grad = lax.dot_general(
        cotangent, weight, (((1,), (1,)), ((), ())), preferred_element_type=jnp.float32
    ).astype(jnp.bfloat16)
    return (keys, input_grad, weight_grad)


def solution(mesh):
    placed = (P(AXES, None), P(("node", "wide"), None), P(AXES, None))
    return jax.shard_map(
        on_device,
        mesh=mesh,
        in_specs=placed,
        out_specs=(P(AXES, None), P(AXES, None), P(("node", "wide"), None)),
        check_vma=False,
    )
```

```python
import functools

import jax
import jax.numpy as jnp
from jax import lax
from jax.experimental import pallas as pl
from jax.experimental.pallas import tpu as pltpu
from jax.sharding import PartitionSpec as P

AXES = ("wide", "node")
TOP = 14.0
NOTE = 8


def products_kernel(place, tok, cot, weight, *rest, first, last):
    keys_in, keys, grad, total = (None if first else rest[0]), *rest[-3:]
    step = pl.program_id(0)

    @pl.when(step == 0)
    def _():
        total[...] = jnp.zeros_like(total) if first else keys_in[...]

    total[...] += jnp.dot(tok[...], weight[0], preferred_element_type=jnp.float32)
    grad[...] = lax.dot_general(
        cot[...], weight[0], (((1,), (1,)), ((), ())), preferred_element_type=jnp.float32
    ).astype(grad.dtype)

    @pl.when(step == pl.num_programs(0) - 1)
    def _():
        keys[...] = total[...].astype(keys.dtype)


def products(tokens, cotangent, weight, z_me, start, before, last):
    steps, depth, kd = weight.shape
    rows = tokens.shape[0]
    whole = pl.BlockSpec((rows, kd), lambda i, z: (0, 0))
    columns = pl.BlockSpec((rows, depth), lambda i, z: (0, z[0] ^ (start + i)))
    in_specs = [columns, whole, pl.BlockSpec((1, depth, kd), lambda i, z: (i, 0, 0))]
    operands = [tokens, cotangent, weight]
    aliases = {}
    if before is not None:
        in_specs += [whole, pl.BlockSpec(memory_space=pl.ANY)]
        operands += list(before)
        aliases = {5: 1}
    return pl.pallas_call(
        functools.partial(products_kernel, first=before is None, last=last),
        grid_spec=pltpu.PrefetchScalarGridSpec(
            num_scalar_prefetch=1,
            grid=(steps,),
            in_specs=in_specs,
            out_specs=[whole, columns],
            scratch_shapes=[pltpu.VMEM((rows, kd), jnp.float32)],
        ),
        out_shape=[
            jax.ShapeDtypeStruct((rows, kd), jnp.bfloat16 if last else jnp.float32),
            jax.ShapeDtypeStruct(tokens.shape, jnp.bfloat16),
        ],
        input_output_aliases=aliases,
        compiler_params=pltpu.CompilerParams(vmem_limit_bytes=24 * 1024 * 1024),
        cost_estimate=pl.CostEstimate(
            flops=4 * rows * steps * depth * kd,
            bytes_accessed=2 * (2 * rows * steps * depth + steps * depth * kd + 3 * rows * kd),
            transcendentals=0,
        ),
    )(jnp.reshape(z_me, (1,)), *operands)


def on_device(tokens, key_weight, cotangent):
    wide, node = lax.axis_size("wide"), lax.axis_size("node")
    w_me, n_me = lax.axis_index("wide"), lax.axis_index("node")
    rows, kd = key_weight.shape
    half = rows // 2
    ny, nx, nz = wide // 2, 2, node // 2
    core, y_me = w_me & 1, w_me >> 1
    x_me, z_me = n_me & 1, n_me >> 1

    def swap(value, name, j):
        mask = {"core": j * node, "y": 2 * j * node, "x": j, "z": 2 * j}[name]
        return lax.ppermute(value, AXES, [(i, i ^ mask) for i in range(wide * node)])

    def gathered(value, name, size, me):
        parts = [value] + [swap(value, name, j) for j in range(1, size)]
        out = jnp.zeros((size,) + value.shape, value.dtype)
        for j in range(size):
            out = lax.dynamic_update_index_in_dim(out, parts[j], me ^ j, 0)
        return out

    def pick(value, axis, index):
        return lax.dynamic_index_in_dim(value, index, axis, keepdims=False)

    def spread(blocks):
        blocks = jnp.stack(blocks).reshape(-1, 2, half, kd)
        one = gathered(gathered(blocks[:, 0], "x", nx, x_me), "y", ny, y_me)
        two = gathered(gathered(blocks[:, 1], "y", ny, y_me), "x", nx, x_me)
        both = jnp.stack([one.transpose(2, 1, 0, 3, 4), two.transpose(2, 0, 1, 3, 4)], axis=3)
        weight = gathered(both, "core", 2, core)
        return weight.transpose(1, 2, 3, 0, 4, 5, 6).reshape(-1, nx * ny * 2 * rows, kd)

    shards = [key_weight] + [swap(key_weight, "z", j) for j in range(1, nz)]
    near = spread(shards[: nz // 2])
    far = spread(shards[nz // 2 :])

    part = lax.dot_general(
        tokens, cotangent, (((0,), (0,)), ((), ())), preferred_element_type=jnp.float32
    )
    top = jnp.maximum(jnp.max(jnp.abs(part), axis=0, keepdims=True), 2.0**-100)
    power = jnp.ceil(jnp.log2(top))
    part = part.reshape(2, nz // 2, nx, ny, 2, rows, kd)

    notes = {}

    def traded(value, power, name, j, key):
        flat = (value.reshape(-1, kd) * jnp.exp2(TOP - power)).astype(jnp.float16)
        if key not in notes:
            note = jnp.broadcast_to(power, (NOTE, kd)).astype(jnp.float16)
            got = swap(jnp.concatenate([flat, note]), name, j)
            notes[key] = got[-NOTE:][:1].astype(jnp.float32)
            got = got[:-NOTE]
        else:
            got = swap(flat, name, j)
        return (got.astype(jnp.float32) * jnp.exp2(notes[key] - TOP)).reshape(value.shape)

    def summed(value, power, axis, name, size, me, key):
        total, bound = pick(value, axis, me), power
        for j in range(1, size):
            total = total + traded(pick(value, axis, me ^ j), power, name, j, (key, j))
            bound = jnp.maximum(bound, notes[key, j])
        return total, bound + (size - 1).bit_length()

    def reduced(slab, power):
        slab, power = summed(slab, power, 3, "core", 2, core, "core")
        one, one_power = summed(slab[:, :, :, :half], power, 1, "x", nx, x_me, "x one")
        two, two_power = summed(slab[:, :, :, half:], power, 2, "y", ny, y_me, "y two")
        one, one_power = summed(one, one_power, 1, "y", ny, y_me, "y one")
        two, two_power = summed(two, two_power, 1, "x", nx, x_me, "x two")
        return jnp.concatenate([one, two], axis=1), jnp.maximum(one_power, two_power)

    z_top = z_me // (nz // 2)
    z_low = z_me % (nz // 2)
    away, power_z = reduced(pick(part, 0, 1 - z_top), power)
    home, power_z = reduced(pick(part, 0, z_top), power)
    total = pick(home, 0, z_low)
    for j in range(nz // 2, nz):
        total = total + traded(pick(away, 0, z_low ^ (j - nz // 2)), power_z, "z", j, ("z", j))
    for j in range(1, nz // 2):
        total = total + traded(pick(home, 0, z_low ^ j), power_z, "z", j, ("z", j))
    total_tokens = tokens.shape[0] * wide * node
    weight_grad = total * (1.0 / jnp.sqrt(jnp.float32(total_tokens)))

    begun = products(tokens, cotangent, near, z_me, 0, None, False)
    keys, input_grad = products(tokens, cotangent, far, z_me, nz // 2, begun, True)
    return (keys, input_grad, weight_grad)


def solution(mesh):
    placed = (P(AXES, None), P(("node", "wide"), None), P(AXES, None))
    return jax.shard_map(
        on_device,
        mesh=mesh,
        in_specs=placed,
        out_specs=(P(AXES, None), P(AXES, None), P(("node", "wide"), None)),
        check_vma=False,
    )
```

```python
import functools

import jax
import jax.numpy as jnp
from jax import lax
from jax.experimental import pallas as pl
from jax.experimental.pallas import tpu as pltpu
from jax.sharding import PartitionSpec as P

AXES = ("wide", "node")
TOP = 14.0


def products_kernel(place, tok, cot, weight, *rest, first, last):
    keys_in, keys, grad, total = (None if first else rest[0]), *rest[-3:]
    step = pl.program_id(0)

    @pl.when(step == 0)
    def _():
        total[...] = jnp.zeros_like(total) if first else keys_in[...]

    total[...] += jnp.dot(tok[...], weight[0], preferred_element_type=jnp.float32)
    grad[...] = lax.dot_general(
        cot[...], weight[0], (((1,), (1,)), ((), ())), preferred_element_type=jnp.float32
    ).astype(grad.dtype)

    @pl.when(step == pl.num_programs(0) - 1)
    def _():
        keys[...] = total[...].astype(keys.dtype)


def products(tokens, cotangent, weight, z_me, start, before, last):
    steps, depth, kd = weight.shape
    rows = tokens.shape[0]
    whole = pl.BlockSpec((rows, kd), lambda i, z: (0, 0))
    columns = pl.BlockSpec((rows, depth), lambda i, z: (0, z[0] ^ (start + i)))
    in_specs = [columns, whole, pl.BlockSpec((1, depth, kd), lambda i, z: (i, 0, 0))]
    operands = [tokens, cotangent, weight]
    aliases = {}
    if before is not None:
        in_specs += [whole, pl.BlockSpec(memory_space=pl.ANY)]
        operands += list(before)
        aliases = {5: 1}
    return pl.pallas_call(
        functools.partial(products_kernel, first=before is None, last=last),
        grid_spec=pltpu.PrefetchScalarGridSpec(
            num_scalar_prefetch=1,
            grid=(steps,),
            in_specs=in_specs,
            out_specs=[whole, columns],
            scratch_shapes=[pltpu.VMEM((rows, kd), jnp.float32)],
        ),
        out_shape=[
            jax.ShapeDtypeStruct((rows, kd), jnp.bfloat16 if last else jnp.float32),
            jax.ShapeDtypeStruct(tokens.shape, jnp.bfloat16),
        ],
        input_output_aliases=aliases,
        compiler_params=pltpu.CompilerParams(vmem_limit_bytes=24 * 1024 * 1024),
        cost_estimate=pl.CostEstimate(
            flops=4 * rows * steps * depth * kd,
            bytes_accessed=2 * (2 * rows * steps * depth + steps * depth * kd + 3 * rows * kd),
            transcendentals=0,
        ),
    )(jnp.reshape(z_me, (1,)), *operands)


def on_device(tokens, key_weight, cotangent):
    wide, node = lax.axis_size("wide"), lax.axis_size("node")
    w_me, n_me = lax.axis_index("wide"), lax.axis_index("node")
    rows, kd = key_weight.shape
    half = rows // 2
    ny, nx, nz = wide // 2, 2, node // 2
    core, y_me = w_me & 1, w_me >> 1
    x_me, z_me = n_me & 1, n_me >> 1

    size = {"core": 2, "y": ny, "x": nx, "z": nz}
    place = {"core": core, "y": y_me, "x": x_me, "z": z_me}
    mask = {"core": node, "y": 2 * node, "x": 1, "z": 2}

    def swap(value, name, j):
        return lax.ppermute(value, AXES, [(i, i ^ (j * mask[name])) for i in range(wide * node)])

    def pick(value, *places):
        start, extent = [0] * value.ndim, list(value.shape)
        for axis, index, *more in places:
            start[axis], extent[axis] = index, (more[0] if more else 1)
        return lax.dynamic_slice(value, start, extent)

    together = lax.optimization_barrier

    def from_all(value, name):
        return [swap(value, name, j) for j in range(1, size[name])]

    def in_order(value, others, name):
        out = jnp.zeros((size[name],) + value.shape, value.dtype)
        for j, part in enumerate([value, *others]):
            out = lax.dynamic_update_index_in_dim(out, part, place[name] ^ j, 0)
        return out

    def top_of(power, name):
        bit = 1
        while bit < size[name]:
            power = jnp.maximum(power, swap(power, name, bit)) + 1.0
            bit *= 2
        return power

    def trade(value, name, axis, *places):
        me = place[name]
        own = pick(value, *places, (axis, me))
        return own, [
            swap(pick(value, *places, (axis, me ^ j)), name, j) for j in range(1, size[name])
        ]

    def added(own, others):
        return sum((other.astype(jnp.float32) for other in others), own.astype(jnp.float32))

    shards = [key_weight] + from_all(key_weight, "z")

    part = lax.dot_general(
        tokens, cotangent, (((0,), (0,)), ((), ())), preferred_element_type=jnp.float32
    )
    top = jnp.maximum(jnp.max(jnp.abs(part), axis=0, keepdims=True), 2.0**-100)
    power = jnp.broadcast_to(jnp.ceil(jnp.log2(top)), (8, kd))
    part = part.reshape(nz, nx, ny, 2, rows, kd)
    z_low = z_me % (nz // 2)
    z_top = z_me - z_low
    z_away = nz // 2 - z_top

    def row(power, factor=1.0):
        return factor * jnp.exp2(power[:1])

    def core_term(first_z, core):
        return pick(part, (0, first_z, nz // 2), (3, core))

    def packed(value):
        return (value * row(TOP - power)).astype(jnp.float16)

    power, shards[1] = together((power, shards[1]))
    power_core = swap(power, "core", 1)
    power_x = top_of(jnp.maximum(power, power_core) + 1.0, "x")
    power_x, shards[nz // 2 :] = together((power_x, shards[nz // 2 :]))
    power_xy = top_of(power_x, "y")
    power_z = top_of(power_xy, "z")

    def chip_sum(own, other):
        total = own + other.astype(jnp.float32) * row(power_core - TOP)
        return (total * row(TOP - power_xy)).astype(jnp.float16)

    upper, lower = (4, 0, half), (4, half, half)

    def near_halves(blocks):
        blocks = jnp.stack(blocks).reshape(-1, 2, half, kd)
        one, two = blocks[:, 0], blocks[:, 1]
        return (one, from_all(one, "x")), (two, from_all(two, "y"))

    def far_halves(one, two):
        one, two = in_order(*one, "x"), in_order(*two, "y")
        return (one, from_all(one, "y")), (two, from_all(two, "x"))

    def joined(one, two):
        one, two = in_order(*one, "y"), in_order(*two, "x")
        both = jnp.stack([one.transpose(2, 1, 0, 3, 4), two.transpose(2, 0, 1, 3, 4)], axis=3)
        return both, from_all(both, "core")

    def whole(both, other):
        weight = in_order(both, other, "core")
        return weight.transpose(1, 2, 3, 0, 4, 5, 6).reshape(-1, nx * ny * 2 * rows, kd)

    def first_sums(total):
        return trade(total, "x", 1, upper), trade(total, "y", 2, lower)

    def second_sums(one, two):
        one = added(*one).astype(jnp.float16)
        two = added(*two).astype(jnp.float16)
        return trade(one, "y", 2), trade(two, "x", 1)

    def last_sums(one, two):
        total = jnp.concatenate([added(*one), added(*two)], axis=4).reshape(-1, rows, kd)
        return (total * row(power_xy - power_z)).astype(jnp.float16)

    away_got = swap(packed(core_term(z_away, 1 - core)), "core", 1)
    near_1 = near_halves(shards[: nz // 2])
    near_2 = far_halves(*near_1)
    away_got, home_sent = together((away_got, packed(core_term(z_top, 1 - core))))
    home_got = swap(home_sent, "core", 1)
    away_total = chip_sum(core_term(z_away, core), away_got)
    away_total, far_shards = together((away_total, shards[nz // 2 :]))
    away_1 = first_sums(away_total)
    far_1 = near_halves(far_shards)
    near_3 = joined(*near_2)
    away_2 = second_sums(*away_1)
    away_2, far_1, home_got = together((away_2, far_1, home_got))
    far_2 = far_halves(*far_1)
    home_1 = first_sums(chip_sum(core_term(z_top, core), home_got))
    begun = products(tokens, cotangent, whole(*near_3), z_me, 0, None, False)
    away_2, begun = together((away_2, begun))
    away_3 = last_sums(*away_2)
    away_sent = [pick(away_3, (0, z_low ^ j)) for j in range(nz // 2)]
    home_1, away_sent = together((home_1, away_sent))
    far_got = [swap(sent, "z", nz // 2 + j) for j, sent in enumerate(away_sent)]
    home_2 = second_sums(*home_1)
    far_3, begun = together((joined(*far_2), begun))
    home_3 = last_sums(*home_2)
    near_got = [swap(pick(home_3, (0, z_low ^ j)), "z", j) for j in range(1, nz // 2)]
    keys, input_grad = products(tokens, cotangent, whole(*far_3), z_me, nz // 2, begun, True)
    total = added(pick(home_3, (0, z_low)), near_got + far_got)[0]
    total_tokens = tokens.shape[0] * wide * node
    weight_grad = total * row(power_z - TOP, 1.0 / jnp.sqrt(jnp.float32(total_tokens)))
    return (keys, input_grad, weight_grad)


def solution(mesh):
    placed = (P(AXES, None), P(("node", "wide"), None), P(AXES, None))
    return jax.shard_map(
        on_device,
        mesh=mesh,
        in_specs=placed,
        out_specs=(P(AXES, None), P(AXES, None), P(("node", "wide"), None)),
        check_vma=False,
    )
```

```python
import jax
import jax.numpy as jnp
from jax import lax
from jax.experimental import pallas as pl
from jax.experimental.pallas import tpu as pltpu
from jax.sharding import PartitionSpec as P

AXES = ("wide", "node")
TOP = 14.0
NOTE = 8


def products_kernel(tok, cot, weight, keys, grad, total):
    step = pl.program_id(0)

    @pl.when(step == 0)
    def _():
        total[...] = jnp.zeros_like(total)

    total[...] += jnp.dot(tok[...], weight[0], preferred_element_type=jnp.float32)
    grad[...] = lax.dot_general(
        cot[...], weight[0], (((1,), (1,)), ((), ())), preferred_element_type=jnp.float32
    ).astype(grad.dtype)

    @pl.when(step == pl.num_programs(0) - 1)
    def _():
        keys[...] = total[...].astype(keys.dtype)


def products(tokens, cotangent, weight):
    steps, depth, kd = weight.shape
    rows = tokens.shape[0]
    whole = pl.BlockSpec((rows, kd), lambda i: (0, 0))
    columns = pl.BlockSpec((rows, depth), lambda i: (0, i))
    return pl.pallas_call(
        products_kernel,
        grid=(steps,),
        in_specs=[columns, whole, pl.BlockSpec((1, depth, kd), lambda i: (i, 0, 0))],
        out_specs=[whole, columns],
        scratch_shapes=[pltpu.VMEM((rows, kd), jnp.float32)],
        out_shape=[
            jax.ShapeDtypeStruct((rows, kd), jnp.bfloat16),
            jax.ShapeDtypeStruct(tokens.shape, jnp.bfloat16),
        ],
        compiler_params=pltpu.CompilerParams(vmem_limit_bytes=24 * 1024 * 1024),
        cost_estimate=pl.CostEstimate(
            flops=4 * rows * steps * depth * kd,
            bytes_accessed=2 * (2 * rows * steps * depth + steps * depth * kd + 3 * rows * kd),
            transcendentals=0,
        ),
    )(tokens, cotangent, weight)


def on_device(tokens, key_weight, cotangent):
    wide, node = lax.axis_size("wide"), lax.axis_size("node")
    w_me, n_me = lax.axis_index("wide"), lax.axis_index("node")
    rows, kd = key_weight.shape
    half = rows // 2
    ny, nx, nz = wide // 2, 2, node // 2
    core, y_me = w_me & 1, w_me >> 1
    x_me, z_me = n_me & 1, n_me >> 1

    size = {"core": 2, "y": ny, "x": nx, "z": nz}
    place = {"core": core, "y": y_me, "x": x_me, "z": z_me}
    mask = {"core": node, "y": 2 * node, "x": 1, "z": 2}

    def swap(value, name, j):
        return lax.ppermute(value, AXES, [(i, i ^ (j * mask[name])) for i in range(wide * node)])

    def pick(value, *places):
        start, extent = [0] * value.ndim, list(value.shape)
        for axis, index, *more in places:
            start[axis], extent[axis] = index, (more[0] if more else 1)
        return lax.dynamic_slice(value, start, extent)

    def in_order(value, others, name):
        out = jnp.zeros((size[name],) + value.shape, value.dtype)
        for j, part in enumerate([value, *others]):
            out = lax.dynamic_update_index_in_dim(out, part, place[name] ^ j, 0)
        return out

    def noted(value, power):
        note = jnp.broadcast_to(power, (NOTE, kd)).astype(value.dtype)
        return jnp.concatenate([value.reshape(-1, kd), note])

    def read(got, shape):
        return got[:-NOTE].reshape(shape), got[-NOTE:][:1].astype(jnp.float32)

    def gathered(value, name, power):
        message = noted(value, power)
        got = [read(swap(message, name, j), value.shape) for j in range(1, size[name])]
        return in_order(value, [one for one, _ in got], name), [other for _, other in got]

    def scale(power):
        return jnp.exp2(power)

    def bound(power, others):
        for other in others:
            power = jnp.maximum(power, other)
        return power + len(others).bit_length()

    def sums(value, name, axis, power, others):
        me = place[name]
        got = [swap(pick(value, (axis, me ^ j)), name, j) for j in range(1, size[name])]
        top = bound(power, others)
        total = pick(value, (axis, me)).astype(jnp.float32) * scale(power - top)
        for one, other in zip(got, others):
            total = total + one.astype(jnp.float32) * scale(other - top)
        return total.astype(jnp.float16), top

    shards = in_order(key_weight, [swap(key_weight, "z", j) for j in range(1, nz)], "z")

    part = lax.dot_general(
        tokens, cotangent, (((0,), (0,)), ((), ())), preferred_element_type=jnp.float32
    )
    top = jnp.maximum(jnp.max(jnp.abs(part), axis=0, keepdims=True), 2.0**-100)
    power = jnp.ceil(jnp.log2(top))
    part = (part * scale(TOP - power)).astype(jnp.float16).reshape(nz * nx * ny, 2, rows, kd)
    power_2 = swap(jnp.broadcast_to(power, (NOTE, kd)), "core", 1)[:1]
    part, power = sums(part, "core", 1, power, [power_2])
    part = part.reshape(nz, nx, ny, 2, half, kd)

    blocks = shards.reshape(nz, 2, half, kd)
    one, power_x = gathered(blocks[:, 0], "x", power)
    two, power_y = gathered(blocks[:, 1], "y", power)
    part, one, two = lax.optimization_barrier((part, one, two))
    sum_one, top_one = sums(part[:, :, :, 0], "x", 1, power, power_x)
    sum_two, top_two = sums(part[:, :, :, 1], "y", 2, power, power_y)
    one, power_xy = gathered(one, "y", top_one)
    two, power_yx = gathered(two, "x", top_two)
    sum_one, top_one = sums(sum_one, "y", 2, top_one, power_xy)
    sum_two, top_two = sums(sum_two, "x", 1, top_two, power_yx)
    both = jnp.stack([one.transpose(2, 1, 0, 3, 4), two.transpose(2, 0, 1, 3, 4)], axis=3)
    weight = in_order(both, [swap(both, "core", 1)], "core")
    weight = weight.transpose(1, 2, 3, 0, 4, 5, 6).reshape(nz, nx * ny * 2 * rows, kd)

    total = jnp.concatenate([sum_one, sum_two], axis=3).reshape(nz, rows, kd)
    got = [
        read(swap(noted(pick(total, (0, z_me ^ j)), top_one), "z", j), (rows, kd))
        for j in range(1, nz)
    ]
    keys, input_grad = products(tokens, cotangent, weight)
    total = pick(total, (0, z_me))[0].astype(jnp.float32) * scale(top_one - TOP)
    for one, other in got:
        total = total + one.astype(jnp.float32) * scale(other - TOP)
    total_tokens = tokens.shape[0] * wide * node
    weight_grad = total * (1.0 / jnp.sqrt(jnp.float32(total_tokens)))
    return (keys, input_grad, weight_grad)


def solution(mesh):
    placed = (P(AXES, None), P(("node", "wide"), None), P(AXES, None))
    return jax.shard_map(
        on_device,
        mesh=mesh,
        in_specs=placed,
        out_specs=(P(AXES, None), P(AXES, None), P(("node", "wide"), None)),
        check_vma=False,
    )
```

```python
import jax
import jax.numpy as jnp
from jax import lax
from jax.experimental import pallas as pl
from jax.experimental.pallas import tpu as pltpu
from jax.sharding import PartitionSpec as P

AXES = ("wide", "node")
TOP = 14.0
NOTE = 8


def products_kernel(tok, cot, weight, keys, grad, total):
    step = pl.program_id(0)

    @pl.when(step == 0)
    def _():
        total[...] = jnp.zeros_like(total)

    total[...] += jnp.dot(tok[...], weight[0], preferred_element_type=jnp.float32)
    grad[...] = lax.dot_general(
        cot[...], weight[0], (((1,), (1,)), ((), ())), preferred_element_type=jnp.float32
    ).astype(grad.dtype)

    @pl.when(step == pl.num_programs(0) - 1)
    def _():
        keys[...] = total[...].astype(keys.dtype)


def products(tokens, cotangent, weight):
    steps, depth, kd = weight.shape
    rows = tokens.shape[0]
    whole = pl.BlockSpec((rows, kd), lambda i: (0, 0))
    columns = pl.BlockSpec((rows, depth), lambda i: (0, i))
    return pl.pallas_call(
        products_kernel,
        grid=(steps,),
        in_specs=[columns, whole, pl.BlockSpec((1, depth, kd), lambda i: (i, 0, 0))],
        out_specs=[whole, columns],
        scratch_shapes=[pltpu.VMEM((rows, kd), jnp.float32)],
        out_shape=[
            jax.ShapeDtypeStruct((rows, kd), jnp.bfloat16),
            jax.ShapeDtypeStruct(tokens.shape, jnp.bfloat16),
        ],
        compiler_params=pltpu.CompilerParams(vmem_limit_bytes=24 * 1024 * 1024),
        cost_estimate=pl.CostEstimate(
            flops=4 * rows * steps * depth * kd,
            bytes_accessed=2 * (2 * rows * steps * depth + steps * depth * kd + 3 * rows * kd),
            transcendentals=0,
        ),
    )(tokens, cotangent, weight)


def bound_kernel(tok, cot, power, total):
    step = pl.program_id(0)

    @pl.when(step == 0)
    def _():
        total[...] = jnp.zeros_like(total)

    reach = jnp.max(jnp.abs(tok[...]).astype(jnp.float32), axis=1, keepdims=True)
    terms = reach * jnp.abs(cot[...]).astype(jnp.float32)
    total[...] += jnp.sum(terms.reshape(-1, NOTE, terms.shape[1]), axis=0)

    @pl.when(step == pl.num_programs(0) - 1)
    def _():
        top = jnp.maximum(jnp.sum(total[...], axis=0, keepdims=True), 2.0**-100)
        power[...] = jnp.broadcast_to(jnp.ceil(jnp.log2(top)), power.shape)


def bound_of(tokens, cotangent):
    rows, width = tokens.shape
    kd = cotangent.shape[1]
    block = min(rows, 128)
    return pl.pallas_call(
        bound_kernel,
        grid=(rows // block,),
        in_specs=[
            pl.BlockSpec((block, width), lambda i: (i, 0)),
            pl.BlockSpec((block, kd), lambda i: (i, 0)),
        ],
        out_specs=pl.BlockSpec((NOTE, kd), lambda i: (0, 0)),
        scratch_shapes=[pltpu.VMEM((NOTE, kd), jnp.float32)],
        out_shape=jax.ShapeDtypeStruct((NOTE, kd), jnp.float32),
        compiler_params=pltpu.CompilerParams(vmem_limit_bytes=40 * 1024 * 1024),
        cost_estimate=pl.CostEstimate(
            flops=2 * rows * width, bytes_accessed=2 * rows * (width + kd), transcendentals=0
        ),
    )(tokens, cotangent)


def on_device(tokens, key_weight, cotangent):
    wide, node = lax.axis_size("wide"), lax.axis_size("node")
    w_me, n_me = lax.axis_index("wide"), lax.axis_index("node")
    rows, kd = key_weight.shape
    half = rows // 2
    ny, nx, nz = wide // 2, 2, node // 2
    core, y_me = w_me & 1, w_me >> 1
    x_me, z_me = n_me & 1, n_me >> 1

    size = {"core": 2, "y": ny, "x": nx, "z": nz}
    place = {"core": core, "y": y_me, "x": x_me, "z": z_me}
    mask = {"core": node, "y": 2 * node, "x": 1, "z": 2}

    def swap(value, name, j):
        return lax.ppermute(value, AXES, [(i, i ^ (j * mask[name])) for i in range(wide * node)])

    def pick(value, *places):
        start, extent = [0] * value.ndim, list(value.shape)
        for axis, index, *more in places:
            start[axis], extent[axis] = index, (more[0] if more else 1)
        return lax.dynamic_slice(value, start, extent)

    def in_order(value, others, name):
        out = jnp.zeros((size[name],) + value.shape, value.dtype)
        for j, part in enumerate([value, *others]):
            out = lax.dynamic_update_index_in_dim(out, part, place[name] ^ j, 0)
        return out

    def noted(value, power):
        note = jnp.broadcast_to(power, (NOTE, kd)).astype(value.dtype)
        return jnp.concatenate([value.reshape(-1, kd), note])

    def read(got, shape):
        return got[:-NOTE].reshape(shape), got[-NOTE:][:1].astype(jnp.float32)

    def gathered(value, name, power):
        message = noted(value, power)
        got = [read(swap(message, name, j), value.shape) for j in range(1, size[name])]
        return in_order(value, [one for one, _ in got], name), [other for _, other in got]

    def scale(power):
        return jnp.exp2(power)

    def bound(power, others):
        for other in others:
            power = jnp.maximum(power, other)
        return power + len(others).bit_length()

    def sums(value, name, axis, power, others):
        me = place[name]
        got = [swap(pick(value, (axis, me ^ j)), name, j) for j in range(1, size[name])]
        top = bound(power, others)
        total = pick(value, (axis, me)).astype(jnp.float32) * scale(power - top)
        for one, other in zip(got, others):
            total = total + one.astype(jnp.float32) * scale(other - top)
        return total.astype(jnp.float16), top

    shards = [swap(key_weight, "z", j) for j in range(1, nz)]

    power = bound_of(tokens, cotangent)
    power = jnp.maximum(power, swap(power, "core", 1))[:1] + 1.0
    part = lax.dot_general(
        tokens, cotangent, (((0,), (0,)), ((), ())), preferred_element_type=jnp.float32
    )
    part = (part * scale(TOP - power)).astype(jnp.float16).reshape(nz * nx * ny, 2, rows, kd)
    part, shards = lax.optimization_barrier((part, shards))
    shards = in_order(key_weight, shards, "z")
    other = swap(pick(part, (1, 1 - core)), "core", 1)
    part = pick(part, (1, core)).astype(jnp.float32) + other.astype(jnp.float32)
    part = part.astype(jnp.float16)
    part = part.reshape(nz, nx, ny, 2, half, kd)

    blocks = shards.reshape(nz, 2, half, kd)
    one, power_x = gathered(blocks[:, 0], "x", power)
    two, power_y = gathered(blocks[:, 1], "y", power)
    part, one, two = lax.optimization_barrier((part, one, two))
    sum_one, top_one = sums(part[:, :, :, 0], "x", 1, power, power_x)
    sum_two, top_two = sums(part[:, :, :, 1], "y", 2, power, power_y)
    one, power_xy = gathered(one, "y", top_one)
    two, power_yx = gathered(two, "x", top_two)
    sum_one, top_one = sums(sum_one, "y", 2, top_one, power_xy)
    sum_two, top_two = sums(sum_two, "x", 1, top_two, power_yx)
    both = jnp.stack([one.transpose(2, 1, 0, 3, 4), two.transpose(2, 0, 1, 3, 4)], axis=3)
    weight = in_order(both, [swap(both, "core", 1)], "core")
    weight = weight.transpose(1, 2, 3, 0, 4, 5, 6).reshape(nz, nx * ny * 2 * rows, kd)

    total = jnp.concatenate([sum_one, sum_two], axis=3).reshape(nz, rows, kd)
    got = [
        swap(noted(pick(total, (0, z_me ^ j)), top_one), "z", j)
        for j in range(1, nz)
    ]
    keys, input_grad = products(tokens, cotangent, weight)
    keys, input_grad, got = lax.optimization_barrier((keys, input_grad, got))
    got = [read(one, (rows, kd)) for one in got]
    total = pick(total, (0, z_me))[0].astype(jnp.float32) * scale(top_one - TOP)
    for one, other in got:
        total = total + one.astype(jnp.float32) * scale(other - TOP)
    total_tokens = tokens.shape[0] * wide * node
    weight_grad = total * (1.0 / jnp.sqrt(jnp.float32(total_tokens)))
    return (keys, input_grad, weight_grad)


def solution(mesh):
    placed = (P(AXES, None), P(("node", "wide"), None), P(AXES, None))
    return jax.shard_map(
        on_device,
        mesh=mesh,
        in_specs=placed,
        out_specs=(P(AXES, None), P(AXES, None), P(("node", "wide"), None)),
        check_vma=False,
    )
```

```python
import jax
import jax.numpy as jnp
from jax import lax
from jax.experimental import pallas as pl
from jax.experimental.pallas import tpu as pltpu
from jax.sharding import PartitionSpec as P

AXES = ("wide", "node")
TOP = 14.0
NOTE = 8


def products_kernel(tok, cot, weight, keys, grad, total):
    step = pl.program_id(0)

    @pl.when(step == 0)
    def _():
        total[...] = jnp.zeros_like(total)

    total[...] += jnp.dot(tok[...], weight[0], preferred_element_type=jnp.float32)
    grad[...] = lax.dot_general(
        cot[...], weight[0], (((1,), (1,)), ((), ())), preferred_element_type=jnp.float32
    ).astype(grad.dtype)

    @pl.when(step == pl.num_programs(0) - 1)
    def _():
        keys[...] = total[...].astype(keys.dtype)


def products(tokens, cotangent, weight):
    steps, depth, kd = weight.shape
    rows = tokens.shape[0]
    whole = pl.BlockSpec((rows, kd), lambda i: (0, 0))
    columns = pl.BlockSpec((rows, depth), lambda i: (0, i))
    return pl.pallas_call(
        products_kernel,
        grid=(steps,),
        in_specs=[columns, whole, pl.BlockSpec((1, depth, kd), lambda i: (i, 0, 0))],
        out_specs=[whole, columns],
        scratch_shapes=[pltpu.VMEM((rows, kd), jnp.float32)],
        out_shape=[
            jax.ShapeDtypeStruct((rows, kd), jnp.bfloat16),
            jax.ShapeDtypeStruct(tokens.shape, jnp.bfloat16),
        ],
        compiler_params=pltpu.CompilerParams(vmem_limit_bytes=12 * 1024 * 1024),
    )(tokens, cotangent, weight)


def bound_kernel(tok, cot, power, total):
    step = pl.program_id(0)

    @pl.when(step == 0)
    def _():
        total[...] = jnp.zeros_like(total)

    reach = jnp.max(jnp.abs(tok[...]).astype(jnp.float32), axis=1, keepdims=True)
    terms = reach * jnp.abs(cot[...]).astype(jnp.float32)
    total[...] += jnp.sum(terms.reshape(-1, NOTE, terms.shape[1]), axis=0)

    @pl.when(step == pl.num_programs(0) - 1)
    def _():
        top = jnp.maximum(jnp.sum(total[...], axis=0, keepdims=True), 2.0**-100)
        power[...] = jnp.broadcast_to(jnp.ceil(jnp.log2(top)), power.shape)


def bound_of(tokens, cotangent):
    rows, width = tokens.shape
    kd = cotangent.shape[1]
    block = min(rows, 128)
    return pl.pallas_call(
        bound_kernel,
        grid=(rows // block,),
        in_specs=[
            pl.BlockSpec((block, width), lambda i: (i, 0)),
            pl.BlockSpec((block, kd), lambda i: (i, 0)),
        ],
        out_specs=pl.BlockSpec((NOTE, kd), lambda i: (0, 0)),
        scratch_shapes=[pltpu.VMEM((NOTE, kd), jnp.float32)],
        out_shape=jax.ShapeDtypeStruct((NOTE, kd), jnp.float32),
        compiler_params=pltpu.CompilerParams(vmem_limit_bytes=60 * 1024 * 1024),
        cost_estimate=pl.CostEstimate(
            flops=2 * rows * width, bytes_accessed=2 * rows * (width + kd), transcendentals=0
        ),
    )(tokens, cotangent)


def on_device(tokens, key_weight, cotangent):
    wide, node = lax.axis_size("wide"), lax.axis_size("node")
    w_me, n_me = lax.axis_index("wide"), lax.axis_index("node")
    rows, kd = key_weight.shape
    half = rows // 2
    ny, nx, nz = wide // 2, 2, node // 2
    core, y_me = w_me & 1, w_me >> 1
    x_me, z_me = n_me & 1, n_me >> 1

    size = {"core": 2, "y": ny, "x": nx, "z": nz}
    place = {"core": core, "y": y_me, "x": x_me, "z": z_me}
    mask = {"core": node, "y": 2 * node, "x": 1, "z": 2}

    def swap(value, name, j):
        return lax.ppermute(value, AXES, [(i, i ^ (j * mask[name])) for i in range(wide * node)])

    def pick(value, *places):
        start, extent = [0] * value.ndim, list(value.shape)
        for axis, index, *more in places:
            start[axis], extent[axis] = index, (more[0] if more else 1)
        return lax.dynamic_slice(value, start, extent)

    def in_order(value, others, name):
        out = jnp.zeros((size[name],) + value.shape, value.dtype)
        for j, part in enumerate([value, *others]):
            out = lax.dynamic_update_index_in_dim(out, part, place[name] ^ j, 0)
        return out

    def noted(value, power):
        note = jnp.broadcast_to(power, (NOTE, kd)).astype(value.dtype)
        return jnp.concatenate([value.reshape(-1, kd), note])

    def read(got, shape):
        return got[:-NOTE].reshape(shape), got[-NOTE:][:1].astype(jnp.float32)

    def gathered(value, name, power):
        message = noted(value, power)
        got = [read(swap(message, name, j), value.shape) for j in range(1, size[name])]
        return in_order(value, [one for one, _ in got], name), [other for _, other in got]

    def scale(power):
        return jnp.exp2(power)

    def factors(power, others):
        top = power
        for other in others:
            top = jnp.maximum(top, other)
        top = top + len(others).bit_length()
        return top, [scale(one - top) for one in [power, *others]]

    def sums(value, name, axis, factor, *places):
        me = place[name]
        got = [swap(pick(value, (axis, me ^ j), *places), name, j) for j in range(1, size[name])]
        total = pick(value, (axis, me), *places).astype(jnp.float32) * factor[0]
        for one, other in zip(got, factor[1:]):
            total = total + one.astype(jnp.float32) * other
        return total.astype(jnp.float16)

    shards = [swap(key_weight, "z", j) for j in range(1, nz)]

    power, shards[0] = lax.optimization_barrier((bound_of(tokens, cotangent), shards[0]))
    power = jnp.maximum(power, swap(power, "core", 1))[:1] + 1.0
    part = lax.dot_general(
        tokens, cotangent, (((0,), (0,)), ((), ())), preferred_element_type=jnp.float32
    )
    part = (part * scale(TOP - power)).astype(jnp.float16).reshape(nz * nx * ny, 2, rows, kd)
    other = swap(pick(part, (1, 1 - core)), "core", 1)
    part, shards = lax.optimization_barrier((part, shards))
    shards = in_order(key_weight, shards, "z")
    part = pick(part, (1, core)).astype(jnp.float32) + other.astype(jnp.float32)
    part = part.astype(jnp.float16).reshape(nz, nx, ny, rows, kd)

    blocks = shards.reshape(nz, 2, half, kd)
    one, power_x = gathered(blocks[:, 0], "x", power)
    two, power_y = gathered(blocks[:, 1], "y", power)
    by_x, by_y = factors(power, power_x), factors(power, power_y)
    part, one, two, by_x, by_y = lax.optimization_barrier((part, one, two, by_x, by_y))
    sum_one = sums(part, "x", 1, by_x[1], (3, 0, half))
    sum_two = sums(part, "y", 2, by_y[1], (3, half, half))
    one, power_xy = gathered(one, "y", by_x[0])
    two, power_yx = gathered(two, "x", by_y[0])
    by_xy, by_yx = factors(by_x[0], power_xy), factors(by_y[0], power_yx)
    top_one = by_xy[0]
    sum_one = sums(sum_one, "y", 2, by_xy[1])
    sum_two = sums(sum_two, "x", 1, by_yx[1])
    both = jnp.stack([one.transpose(2, 1, 0, 3, 4), two.transpose(2, 0, 1, 3, 4)], axis=3)
    weight = in_order(both, [swap(both, "core", 1)], "core")
    weight = weight.transpose(1, 2, 3, 0, 4, 5, 6).reshape(nz, nx * ny * 2 * rows, kd)

    total = jnp.concatenate([sum_one, sum_two], axis=3).reshape(nz, rows, kd)
    got = [
        swap(noted(pick(total, (0, z_me ^ j)), top_one), "z", j)
        for j in range(1, nz)
    ]
    keys, input_grad = products(tokens, cotangent, weight)
    keys, input_grad, got = lax.optimization_barrier((keys, input_grad, got))
    got = [read(one, (rows, kd)) for one in got]
    total = pick(total, (0, z_me))[0].astype(jnp.float32) * scale(top_one - TOP)
    for one, other in got:
        total = total + one.astype(jnp.float32) * scale(other - TOP)
    total_tokens = tokens.shape[0] * wide * node
    weight_grad = total * (1.0 / jnp.sqrt(jnp.float32(total_tokens)))
    return (keys, input_grad, weight_grad)


def solution(mesh):
    placed = (P(AXES, None), P(("node", "wide"), None), P(AXES, None))
    return jax.shard_map(
        on_device,
        mesh=mesh,
        in_specs=placed,
        out_specs=(P(AXES, None), P(AXES, None), P(("node", "wide"), None)),
        check_vma=False,
    )
```

```python
import jax
import jax.numpy as jnp
from jax import lax
from jax.experimental import pallas as pl
from jax.experimental.pallas import tpu as pltpu
from jax.sharding import PartitionSpec as P

AXES = ("wide", "node")
TOP = 14.0
NOTE = 8


def products_kernel(tok, cot, weight, keys, grad, total):
    step = pl.program_id(0)

    @pl.when(step == 0)
    def _():
        total[...] = jnp.zeros_like(total)

    total[...] += jnp.dot(tok[...], weight[0], preferred_element_type=jnp.float32)
    grad[...] = lax.dot_general(
        cot[...], weight[0], (((1,), (1,)), ((), ())), preferred_element_type=jnp.float32
    ).astype(grad.dtype)

    @pl.when(step == pl.num_programs(0) - 1)
    def _():
        keys[...] = total[...].astype(keys.dtype)


def products(tokens, cotangent, weight):
    steps, depth, kd = weight.shape
    rows = tokens.shape[0]
    whole = pl.BlockSpec((rows, kd), lambda i: (0, 0))
    columns = pl.BlockSpec((rows, depth), lambda i: (0, i))
    return pl.pallas_call(
        products_kernel,
        grid=(steps,),
        in_specs=[columns, whole, pl.BlockSpec((1, depth, kd), lambda i: (i, 0, 0))],
        out_specs=[whole, columns],
        scratch_shapes=[pltpu.VMEM((rows, kd), jnp.float32)],
        out_shape=[
            jax.ShapeDtypeStruct((rows, kd), jnp.bfloat16),
            jax.ShapeDtypeStruct(tokens.shape, jnp.bfloat16),
        ],
        compiler_params=pltpu.CompilerParams(vmem_limit_bytes=12 * 1024 * 1024),
    )(tokens, cotangent, weight)


def bound_kernel(tok, cot, power, total):
    step = pl.program_id(0)
    lanes = 128

    @pl.when(step == 0)
    def _():
        total[...] = jnp.zeros_like(total)

    reach = jnp.abs(tok[:, :lanes])
    for first in range(lanes, tok.shape[1], lanes):
        reach = jnp.maximum(reach, jnp.abs(tok[:, first : first + lanes]))
    reach = jnp.max(reach.astype(jnp.float32), axis=1, keepdims=True)
    terms = reach * jnp.abs(cot[...]).astype(jnp.float32)
    total[...] += jnp.sum(terms.reshape(-1, NOTE, terms.shape[1]), axis=0)

    @pl.when(step == pl.num_programs(0) - 1)
    def _():
        top = jnp.maximum(jnp.sum(total[...], axis=0, keepdims=True), 2.0**-100)
        power[...] = jnp.broadcast_to(jnp.ceil(jnp.log2(top)), power.shape)


def bound_of(tokens, cotangent):
    rows, width = tokens.shape
    kd = cotangent.shape[1]
    block = min(rows, 64)
    return pl.pallas_call(
        bound_kernel,
        grid=(rows // block,),
        in_specs=[
            pl.BlockSpec((block, width), lambda i: (i, 0)),
            pl.BlockSpec((block, kd), lambda i: (i, 0)),
        ],
        out_specs=pl.BlockSpec((NOTE, kd), lambda i: (0, 0)),
        scratch_shapes=[pltpu.VMEM((NOTE, kd), jnp.float32)],
        out_shape=jax.ShapeDtypeStruct((NOTE, kd), jnp.float32),
        compiler_params=pltpu.CompilerParams(vmem_limit_bytes=60 * 1024 * 1024),
        cost_estimate=pl.CostEstimate(
            flops=2 * rows * width, bytes_accessed=2 * rows * (width + kd), transcendentals=0
        ),
    )(tokens, cotangent)


def on_device(tokens, key_weight, cotangent):
    wide, node = lax.axis_size("wide"), lax.axis_size("node")
    w_me, n_me = lax.axis_index("wide"), lax.axis_index("node")
    rows, kd = key_weight.shape
    half = rows // 2
    ny, nx, nz = wide // 2, 2, node // 2
    core, y_me = w_me & 1, w_me >> 1
    x_me, z_me = n_me & 1, n_me >> 1

    size = {"core": 2, "y": ny, "x": nx, "z": nz}
    place = {"core": core, "y": y_me, "x": x_me, "z": z_me}
    mask = {"core": node, "y": 2 * node, "x": 1, "z": 2}

    def swap(value, name, j):
        return lax.ppermute(value, AXES, [(i, i ^ (j * mask[name])) for i in range(wide * node)])

    def pick(value, *places):
        start, extent = [0] * value.ndim, list(value.shape)
        for axis, index, *more in places:
            start[axis], extent[axis] = index, (more[0] if more else 1)
        return lax.dynamic_slice(value, start, extent)

    def in_order(value, others, name):
        out = jnp.zeros((size[name],) + value.shape, value.dtype)
        for j, part in enumerate([value, *others]):
            out = lax.dynamic_update_index_in_dim(out, part, place[name] ^ j, 0)
        return out

    def noted(value, power):
        note = jnp.broadcast_to(power, (NOTE, kd)).astype(value.dtype)
        return jnp.concatenate([value.reshape(-1, kd), note])

    def read(got, shape):
        return got[:-NOTE].reshape(shape), got[-NOTE:][:1].astype(jnp.float32)

    def gathered(value, name, power):
        message = noted(value, power)
        got = [read(swap(message, name, j), value.shape) for j in range(1, size[name])]
        return in_order(value, [one for one, _ in got], name), [other for _, other in got]

    def scale(power):
        return jnp.exp2(power)

    def factors(power, others):
        top = power
        for other in others:
            top = jnp.maximum(top, other)
        top = top + len(others).bit_length()
        return top, [scale(one - top) for one in [power, *others]]

    def given(value, name, axis, *places):
        me = place[name]
        return [swap(pick(value, (axis, me ^ j), *places), name, j) for j in range(1, size[name])]

    def taken(value, got, name, axis, factor, *places):
        total = pick(value, (axis, place[name]), *places).astype(jnp.float32) * factor[0]
        for one, other in zip(got, factor[1:]):
            total = total + one.astype(jnp.float32) * other
        return total.astype(jnp.float16)

    held = lax.optimization_barrier

    shards = [swap(key_weight, "z", j) for j in range(1, nz)]

    power, shards[0] = held((bound_of(tokens, cotangent), shards[0]))
    power = jnp.maximum(power, swap(power, "core", 1))[:1] + 1.0
    part = lax.dot_general(
        tokens, cotangent, (((0,), (0,)), ((), ())), preferred_element_type=jnp.float32
    )
    part = (part * scale(TOP - power)).astype(jnp.float16).reshape(nz, nx, ny, 2, rows, kd)
    z_low = z_me % (nz // 2)
    z_top = z_me - z_low
    far, near = (0, nz // 2 - z_top, nz // 2), (0, z_top, nz // 2)
    far_got = swap(pick(part, far, (3, 1 - core)), "core", 1)
    near_got = swap(pick(part, near, (3, 1 - core)), "core", 1)
    part, shards = held((part, shards))
    shards = in_order(key_weight, shards, "z")

    def pair_sum(where, got):
        total = pick(part, where, (3, core)).astype(jnp.float32) + got.astype(jnp.float32)
        return total.astype(jnp.float16).reshape(nz // 2, nx, ny, rows, kd)

    upper, lower = (3, 0, half), (3, half, half)

    blocks = shards.reshape(nz, 2, half, kd)
    one, power_x = gathered(blocks[:, 0], "x", power)
    two, power_y = gathered(blocks[:, 1], "y", power)
    by_x, by_y = factors(power, power_x), factors(power, power_y)
    far_sum = pair_sum(far, far_got)
    far_one, far_two = given(far_sum, "x", 1, upper), given(far_sum, "y", 2, lower)
    far_sum, one, two, by_x, by_y = held((far_sum, one, two, by_x, by_y))
    one, power_xy = gathered(one, "y", by_x[0])
    two, power_yx = gathered(two, "x", by_y[0])
    by_xy, by_yx = factors(by_x[0], power_xy), factors(by_y[0], power_yx)
    top = by_xy[0]

    far_one = taken(far_sum, far_one, "x", 1, by_x[1], upper)
    far_two = taken(far_sum, far_two, "y", 2, by_y[1], lower)
    far_one_got, far_two_got = given(far_one, "y", 2), given(far_two, "x", 1)
    near_got, far_one, far_two = held((near_got, far_one, far_two))
    near_sum = pair_sum(near, near_got)
    near_one, near_two = given(near_sum, "x", 1, upper), given(near_sum, "y", 2, lower)

    both = jnp.stack([one.transpose(2, 1, 0, 3, 4), two.transpose(2, 0, 1, 3, 4)], axis=3)
    weight = in_order(both, [swap(both, "core", 1)], "core")
    weight = weight.transpose(1, 2, 3, 0, 4, 5, 6).reshape(nz, nx * ny * 2 * rows, kd)

    def last_sum(one, one_got, two, two_got):
        one = taken(one, one_got, "y", 2, by_xy[1])
        two = taken(two, two_got, "x", 1, by_yx[1])
        return jnp.concatenate([one, two], axis=3).reshape(nz // 2, rows, kd)

    far_sum = last_sum(far_one, far_one_got, far_two, far_two_got)
    packets = [noted(pick(far_sum, (0, z_low ^ j)), top) for j in range(nz // 2)]
    near_one = taken(near_sum, near_one, "x", 1, by_x[1], upper)
    near_two = taken(near_sum, near_two, "y", 2, by_y[1], lower)
    later, near_one, near_two = held((packets[nz // 4 :], near_one, near_two))
    packets[nz // 4 :] = later
    got = [swap(packet, "z", nz // 2 + j) for j, packet in enumerate(packets)]
    near_one_got, near_two_got = given(near_one, "y", 2), given(near_two, "x", 1)
    near_sum = last_sum(near_one, near_one_got, near_two, near_two_got)
    got += [swap(noted(pick(near_sum, (0, z_low ^ j)), top), "z", j) for j in range(1, nz // 2)]

    keys, input_grad = products(tokens, cotangent, weight)
    keys, input_grad, got = held((keys, input_grad, got))
    total = pick(near_sum, (0, z_low))[0].astype(jnp.float32) * scale(top - TOP)
    for one, other in [read(one, (rows, kd)) for one in got]:
        total = total + one.astype(jnp.float32) * scale(other - TOP)
    total_tokens = tokens.shape[0] * wide * node
    weight_grad = total * (1.0 / jnp.sqrt(jnp.float32(total_tokens)))
    return (keys, input_grad, weight_grad)


def solution(mesh):
    placed = (P(AXES, None), P(("node", "wide"), None), P(AXES, None))
    return jax.shard_map(
        on_device,
        mesh=mesh,
        in_specs=placed,
        out_specs=(P(AXES, None), P(AXES, None), P(("node", "wide"), None)),
        check_vma=False,
    )
```

```python
import jax
import jax.numpy as jnp
from jax import lax
from jax.experimental import pallas as pl
from jax.experimental.pallas import tpu as pltpu
from jax.sharding import PartitionSpec as P

AXES = ("wide", "node")
TOP = 14.0
NOTE = 8


def products_kernel(tok, cot, weight, keys, grad, total):
    step = pl.program_id(0)

    @pl.when(step == 0)
    def _():
        total[...] = jnp.zeros_like(total)

    total[...] += jnp.dot(tok[...], weight[0], preferred_element_type=jnp.float32)
    grad[...] = lax.dot_general(
        cot[...], weight[0], (((1,), (1,)), ((), ())), preferred_element_type=jnp.float32
    ).astype(grad.dtype)

    @pl.when(step == pl.num_programs(0) - 1)
    def _():
        keys[...] = total[...].astype(keys.dtype)


def products(tokens, cotangent, weight):
    steps, depth, kd = weight.shape
    rows = tokens.shape[0]
    whole = pl.BlockSpec((rows, kd), lambda i: (0, 0))
    columns = pl.BlockSpec((rows, depth), lambda i: (0, i))
    return pl.pallas_call(
        products_kernel,
        grid=(steps,),
        in_specs=[columns, whole, pl.BlockSpec((1, depth, kd), lambda i: (i, 0, 0))],
        out_specs=[whole, columns],
        scratch_shapes=[pltpu.VMEM((rows, kd), jnp.float32)],
        out_shape=[
            jax.ShapeDtypeStruct((rows, kd), jnp.bfloat16),
            jax.ShapeDtypeStruct(tokens.shape, jnp.bfloat16),
        ],
        compiler_params=pltpu.CompilerParams(vmem_limit_bytes=12 * 1024 * 1024),
    )(tokens, cotangent, weight)


def bound_kernel(tok, cot, power, tok_here, cot_here, arrived):
    parts = arrived.shape[0] - 1
    block = tok.shape[0] // parts
    copies = [pltpu.make_async_copy(cot, cot_here, arrived.at[parts])]
    for i in range(parts):
        some = pl.ds(i * block, block)
        copies.append(pltpu.make_async_copy(tok.at[some], tok_here.at[some], arrived.at[i]))
    for copy in copies:
        copy.start()
    copies[0].wait()
    total = jnp.zeros(power.shape, jnp.float32)
    for i in range(parts):
        copies[1 + i].wait()
        some = pl.ds(i * block, block)
        reach = jnp.max(jnp.abs(tok_here[some]).astype(jnp.float32), axis=1, keepdims=True)
        terms = reach * jnp.abs(cot_here[some]).astype(jnp.float32)
        total += jnp.sum(terms.reshape(-1, NOTE, terms.shape[1]), axis=0)
    top = jnp.maximum(jnp.sum(total, axis=0, keepdims=True), 2.0**-100)
    power[...] = jnp.broadcast_to(jnp.ceil(jnp.log2(top)), power.shape)


def bound_of(tokens, cotangent):
    rows, width = tokens.shape
    kd = cotangent.shape[1]
    return pl.pallas_call(
        bound_kernel,
        in_specs=[pl.BlockSpec(memory_space=pl.ANY)] * 2,
        out_specs=pl.BlockSpec(memory_space=pltpu.VMEM),
        scratch_shapes=[
            pltpu.VMEM(tokens.shape, tokens.dtype),
            pltpu.VMEM(cotangent.shape, cotangent.dtype),
            pltpu.SemaphoreType.DMA((max(rows // 128, 1) + 1,)),
        ],
        out_shape=jax.ShapeDtypeStruct((NOTE, kd), jnp.float32),
        compiler_params=pltpu.CompilerParams(vmem_limit_bytes=60 * 1024 * 1024),
        cost_estimate=pl.CostEstimate(
            flops=2 * rows * width, bytes_accessed=2 * rows * (width + kd), transcendentals=0
        ),
    )(tokens, cotangent)


def on_device(tokens, key_weight, cotangent):
    wide, node = lax.axis_size("wide"), lax.axis_size("node")
    w_me, n_me = lax.axis_index("wide"), lax.axis_index("node")
    rows, kd = key_weight.shape
    half = rows // 2
    ny, nx, nz = wide // 2, 2, node // 2
    core, y_me = w_me & 1, w_me >> 1
    x_me, z_me = n_me & 1, n_me >> 1

    size = {"core": 2, "y": ny, "x": nx, "z": nz}
    place = {"core": core, "y": y_me, "x": x_me, "z": z_me}
    mask = {"core": node, "y": 2 * node, "x": 1, "z": 2}

    def swap(value, name, j):
        return lax.ppermute(value, AXES, [(i, i ^ (j * mask[name])) for i in range(wide * node)])

    def pick(value, *places):
        start, extent = [0] * value.ndim, list(value.shape)
        for axis, index, *more in places:
            start[axis], extent[axis] = index, (more[0] if more else 1)
        return lax.dynamic_slice(value, start, extent)

    def in_order(value, others, name):
        out = jnp.zeros((size[name],) + value.shape, value.dtype)
        for j, part in enumerate([value, *others]):
            out = lax.dynamic_update_index_in_dim(out, part, place[name] ^ j, 0)
        return out

    def noted(value, power):
        note = jnp.broadcast_to(power, (NOTE, kd)).astype(value.dtype)
        return jnp.concatenate([value.reshape(-1, kd), note])

    def read(got, shape):
        return got[:-NOTE].reshape(shape), got[-NOTE:][:1].astype(jnp.float32)

    def gathered(value, name, power):
        message = noted(value, power)
        got = [read(swap(message, name, j), value.shape) for j in range(1, size[name])]
        return in_order(value, [one for one, _ in got], name), [other for _, other in got]

    def scale(power):
        return jnp.exp2(power)

    def factors(power, others):
        top = power
        for other in others:
            top = jnp.maximum(top, other)
        top = top + len(others).bit_length()
        return top, [scale(one - top) for one in [power, *others]]

    def given(value, name, axis, *places):
        me = place[name]
        return [swap(pick(value, (axis, me ^ j), *places), name, j) for j in range(1, size[name])]

    def taken(value, got, name, axis, factor, *places):
        total = pick(value, (axis, place[name]), *places).astype(jnp.float32) * factor[0]
        for one, other in zip(got, factor[1:]):
            total = total + one.astype(jnp.float32) * other
        return total.astype(jnp.float16)

    held = lax.optimization_barrier

    shards = [swap(key_weight, "z", j) for j in range(1, nz)]

    power, shards[0] = held((bound_of(tokens, cotangent), shards[0]))
    power = jnp.maximum(power, swap(power, "core", 1))[:1] + 1.0
    part = lax.dot_general(
        tokens, cotangent, (((0,), (0,)), ((), ())), preferred_element_type=jnp.float32
    )
    part = (part * scale(TOP - power)).astype(jnp.float16).reshape(nz, nx, ny, 2, rows, kd)
    z_low = z_me % (nz // 2)
    z_top = z_me - z_low
    far, near = (0, nz // 2 - z_top, nz // 2), (0, z_top, nz // 2)
    upper, lower = (3, 0, half), (3, half, half)
    other = swap(pick(part, (3, 1 - core)), "core", 1)
    part = pick(part, (3, core)).astype(jnp.float32) + other.astype(jnp.float32)
    part = part.astype(jnp.float16).reshape(nz, nx, ny, rows, kd)

    part, power, shards = held((part, power, shards))
    far_one, far_two = given(part, "x", 1, far, upper), given(part, "y", 2, far, lower)
    blocks = in_order(key_weight, shards, "z").reshape(nz, 2, half, kd)
    one, power_x = gathered(blocks[:, 0], "x", power)
    two, power_y = gathered(blocks[:, 1], "y", power)
    by_x, by_y = factors(power, power_x), factors(power, power_y)
    by_x, by_y = held((by_x, by_y))
    one, power_xy = gathered(one, "y", by_x[0])
    two, power_yx = gathered(two, "x", by_y[0])

    far_one = taken(part, far_one, "x", 1, by_x[1], far, upper)
    far_two = taken(part, far_two, "y", 2, by_y[1], far, lower)
    far_one_got, far_two_got = given(far_one, "y", 2), given(far_two, "x", 1)
    part, far_one_got, far_two_got = held((part, far_one_got, far_two_got))
    near_one, near_two = given(part, "x", 1, near, upper), given(part, "y", 2, near, lower)

    by_xy, by_yx = factors(by_x[0], power_xy), factors(by_y[0], power_yx)
    top = by_xy[0]
    both = jnp.stack([one.transpose(2, 1, 0, 3, 4), two.transpose(2, 0, 1, 3, 4)], axis=3)
    weight = in_order(both, [swap(both, "core", 1)], "core")
    weight = weight.transpose(1, 2, 3, 0, 4, 5, 6).reshape(nz, nx * ny * 2 * rows, kd)

    def last_sum(one, one_got, two, two_got):
        one = taken(one, one_got, "y", 2, by_xy[1])
        two = taken(two, two_got, "x", 1, by_yx[1])
        return jnp.concatenate([one, two], axis=3).reshape(nz // 2, rows, kd)

    far_sum = last_sum(far_one, far_one_got, far_two, far_two_got)
    packets = [noted(pick(far_sum, (0, z_low ^ j)), top) for j in range(nz // 2)]
    near_one = taken(part, near_one, "x", 1, by_x[1], near, upper)
    near_two = taken(part, near_two, "y", 2, by_y[1], near, lower)
    packets, near_one, near_two = held((packets, near_one, near_two))
    got = [swap(packet, "z", nz // 2 + j) for j, packet in enumerate(packets)]
    near_one_got, near_two_got = given(near_one, "y", 2), given(near_two, "x", 1)
    near_sum = last_sum(near_one, near_one_got, near_two, near_two_got)
    got += [swap(noted(pick(near_sum, (0, z_low ^ j)), top), "z", j) for j in range(1, nz // 2)]

    keys, input_grad = products(tokens, cotangent, weight)
    keys, input_grad, got = held((keys, input_grad, got))
    total = pick(near_sum, (0, z_low))[0].astype(jnp.float32) * scale(top - TOP)
    for one, other in [read(one, (rows, kd)) for one in got]:
        total = total + one.astype(jnp.float32) * scale(other - TOP)
    total_tokens = tokens.shape[0] * wide * node
    weight_grad = total * (1.0 / jnp.sqrt(jnp.float32(total_tokens)))
    return (keys, input_grad, weight_grad)


def solution(mesh):
    placed = (P(AXES, None), P(("node", "wide"), None), P(AXES, None))
    return jax.shard_map(
        on_device,
        mesh=mesh,
        in_specs=placed,
        out_specs=(P(AXES, None), P(AXES, None), P(("node", "wide"), None)),
        check_vma=False,
    )
```

```python
import jax
import jax.numpy as jnp
from jax import lax
from jax.experimental import pallas as pl
from jax.experimental.pallas import tpu as pltpu
from jax.sharding import PartitionSpec as P

AXES = ("wide", "node")
TOP = 14.0
NOTE = 8


def products_kernel(tok, cot, weight, keys, grad, total):
    step = pl.program_id(0)

    @pl.when(step == 0)
    def _():
        total[...] = jnp.zeros_like(total)

    total[...] += jnp.dot(tok[...], weight[0], preferred_element_type=jnp.float32)
    grad[...] = lax.dot_general(
        cot[...], weight[0], (((1,), (1,)), ((), ())), preferred_element_type=jnp.float32
    ).astype(grad.dtype)

    @pl.when(step == pl.num_programs(0) - 1)
    def _():
        keys[...] = total[...].astype(keys.dtype)


def products(tokens, cotangent, weight):
    steps, depth, kd = weight.shape
    rows = tokens.shape[0]
    whole = pl.BlockSpec((rows, kd), lambda i: (0, 0))
    columns = pl.BlockSpec((rows, depth), lambda i: (0, i))
    return pl.pallas_call(
        products_kernel,
        grid=(steps,),
        in_specs=[columns, whole, pl.BlockSpec((1, depth, kd), lambda i: (i, 0, 0))],
        out_specs=[whole, columns],
        scratch_shapes=[pltpu.VMEM((rows, kd), jnp.float32)],
        out_shape=[
            jax.ShapeDtypeStruct((rows, kd), jnp.bfloat16),
            jax.ShapeDtypeStruct(tokens.shape, jnp.bfloat16),
        ],
        compiler_params=pltpu.CompilerParams(vmem_limit_bytes=12 * 1024 * 1024),
    )(tokens, cotangent, weight)


def bound_kernel(tok, cot, power, tok_here, cot_here, arrived):
    parts = arrived.shape[0] - 1
    block = tok.shape[0] // parts
    copies = [pltpu.make_async_copy(cot, cot_here, arrived.at[parts])]
    for i in range(parts):
        some = pl.ds(i * block, block)
        copies.append(pltpu.make_async_copy(tok.at[some], tok_here.at[some], arrived.at[i]))
    for copy in copies:
        copy.start()
    copies[0].wait()
    total = jnp.zeros(power.shape, jnp.float32)
    for i in range(parts):
        copies[1 + i].wait()
        some = pl.ds(i * block, block)
        reach = jnp.max(jnp.abs(tok_here[some]).astype(jnp.float32), axis=1, keepdims=True)
        terms = reach * jnp.abs(cot_here[some]).astype(jnp.float32)
        total += jnp.sum(terms.reshape(-1, NOTE, terms.shape[1]), axis=0)
    top = jnp.maximum(jnp.sum(total, axis=0, keepdims=True), 2.0**-100)
    power[...] = jnp.broadcast_to(jnp.ceil(jnp.log2(top)), power.shape)


def bound_of(tokens, cotangent):
    rows, width = tokens.shape
    kd = cotangent.shape[1]
    return pl.pallas_call(
        bound_kernel,
        in_specs=[pl.BlockSpec(memory_space=pl.ANY)] * 2,
        out_specs=pl.BlockSpec(memory_space=pltpu.VMEM),
        scratch_shapes=[
            pltpu.VMEM(tokens.shape, tokens.dtype),
            pltpu.VMEM(cotangent.shape, cotangent.dtype),
            pltpu.SemaphoreType.DMA((max(rows // 128, 1) + 1,)),
        ],
        out_shape=jax.ShapeDtypeStruct((NOTE, kd), jnp.float32),
        compiler_params=pltpu.CompilerParams(vmem_limit_bytes=60 * 1024 * 1024),
        cost_estimate=pl.CostEstimate(
            flops=2 * rows * width, bytes_accessed=2 * rows * (width + kd), transcendentals=0
        ),
    )(tokens, cotangent)


def on_device(tokens, key_weight, cotangent):
    wide, node = lax.axis_size("wide"), lax.axis_size("node")
    w_me, n_me = lax.axis_index("wide"), lax.axis_index("node")
    rows, kd = key_weight.shape
    n = wide // 2
    nz = node // n
    core, y_me = w_me & 1, w_me >> 1
    x_me, z_me = n_me % n, n_me // n
    size = {"core": 2, "first": n, "second": n, "z": nz}
    place = {
        "core": core,
        "first": jnp.where(core == 0, x_me, y_me),
        "second": jnp.where(core == 0, y_me, x_me),
        "z": z_me,
    }

    def swap(value, name, j):
        over_x, over_y = 1, 2 * node
        mask = {
            "core": (node, node),
            "first": (over_x, over_y),
            "second": (over_y, over_x),
            "z": (n, n),
        }[name]
        pairs = [(i, i ^ (j * mask[i // node % 2])) for i in range(wide * node)]
        return lax.ppermute(value, AXES, pairs)

    def pick(value, *places):
        start, extent = [0] * value.ndim, list(value.shape)
        for axis, index, *more in places:
            start[axis], extent[axis] = index, (more[0] if more else 1)
        return lax.dynamic_slice(value, start, extent)

    def in_order(value, others, name):
        out = jnp.zeros((size[name],) + value.shape, value.dtype)
        for j, part in enumerate([value, *others]):
            out = lax.dynamic_update_index_in_dim(out, part, place[name] ^ j, 0)
        return out

    def noted(value, power):
        note = jnp.broadcast_to(power, (NOTE, kd)).astype(value.dtype)
        return jnp.concatenate([value.reshape(-1, kd), note])

    def read(got, shape):
        return got[:-NOTE].reshape(shape), got[-NOTE:][:1].astype(jnp.float32)

    def gathered(value, name, power):
        message = noted(value, power)
        got = [read(swap(message, name, j), value.shape) for j in range(1, size[name])]
        return in_order(value, [one for one, _ in got], name), [other for _, other in got]

    def scale(power):
        return jnp.exp2(power)

    def factors(power, others):
        top = power
        for other in others:
            top = jnp.maximum(top, other)
        top = top + len(others).bit_length()
        return top, [scale(one - top) for one in [power, *others]]

    def given(value, name, axis, *places):
        me = place[name]
        return [swap(pick(value, (axis, me ^ j), *places), name, j) for j in range(1, size[name])]

    def taken(value, got, name, axis, factor, *places):
        total = pick(value, (axis, place[name]), *places).astype(jnp.float32) * factor[0]
        for one, other in zip(got, factor[1:]):
            total = total + one.astype(jnp.float32) * other
        return total.astype(jnp.float16)

    held = lax.optimization_barrier

    shards = [swap(key_weight, "z", j) for j in range(1, nz)]

    power, shards[0] = held((bound_of(tokens, cotangent), shards[0]))
    power = jnp.maximum(power, swap(power, "core", 1))[:1] + 1.0
    part = lax.dot_general(
        tokens, cotangent, (((0,), (0,)), ((), ())), preferred_element_type=jnp.float32
    )
    part = (part * scale(TOP - power)).astype(jnp.float16).reshape(nz * n * n, 2, rows, kd)
    other = swap(pick(part, (1, 1 - core)), "core", 1)
    part, shards = held((part, shards))
    blocks = in_order(key_weight, shards, "z")
    part = pick(part, (1, core)).astype(jnp.float32) + other.astype(jnp.float32)
    part = part.astype(jnp.float16).reshape(nz, n, n, rows, kd)
    part = jnp.where(core == 0, part, part.transpose(0, 2, 1, 3, 4))

    blocks, power_first = gathered(blocks, "first", power)
    by_first = factors(power, power_first)
    part, blocks, by_first = held((part, blocks, by_first))
    sums = taken(part, given(part, "first", 1), "first", 1, by_first[1])
    blocks, power_second = gathered(blocks, "second", by_first[0])
    by_second = factors(by_first[0], power_second)
    sums = taken(sums, given(sums, "second", 2), "second", 2, by_second[1])
    sums = sums.reshape(nz, rows, kd)

    other = swap(blocks, "core", 1)
    x_first = jnp.where(core == 0, blocks, other).transpose(2, 1, 0, 3, 4)
    y_first = jnp.where(core == 0, other, blocks).transpose(2, 0, 1, 3, 4)
    weight = jnp.stack([x_first, y_first], axis=3).reshape(nz, n * n * 2 * rows, kd)

    top = by_second[0]
    got = [swap(noted(pick(sums, (0, z_me ^ j)), top), "z", j) for j in range(1, nz)]
    keys, input_grad = products(tokens, cotangent, weight)
    keys, input_grad, got = held((keys, input_grad, got))
    total = pick(sums, (0, z_me))[0].astype(jnp.float32) * scale(top - TOP)
    for one, other in [read(one, (rows, kd)) for one in got]:
        total = total + one.astype(jnp.float32) * scale(other - TOP)
    total_tokens = tokens.shape[0] * wide * node
    weight_grad = total * (1.0 / jnp.sqrt(jnp.float32(total_tokens)))
    return (keys, input_grad, weight_grad)


def solution(mesh):
    placed = (P(AXES, None), P(("node", "wide"), None), P(AXES, None))
    return jax.shard_map(
        on_device,
        mesh=mesh,
        in_specs=placed,
        out_specs=(P(AXES, None), P(AXES, None), P(("node", "wide"), None)),
        check_vma=False,
    )
```

```python
import jax
import jax.numpy as jnp
from jax import lax
from jax.experimental import pallas as pl
from jax.experimental.pallas import tpu as pltpu
from jax.sharding import PartitionSpec as P

AXES = ("wide", "node")
TOP = 14.0
NOTE = 8


def products_kernel(tok, cot, weight, keys, grad, total):
    step = pl.program_id(0)

    @pl.when(step == 0)
    def _():
        total[...] = jnp.zeros_like(total)

    total[...] += jnp.dot(tok[...], weight[0], preferred_element_type=jnp.float32)
    grad[...] = lax.dot_general(
        cot[...], weight[0], (((1,), (1,)), ((), ())), preferred_element_type=jnp.float32
    ).astype(grad.dtype)

    @pl.when(step == pl.num_programs(0) - 1)
    def _():
        keys[...] = total[...].astype(keys.dtype)


def products(tokens, cotangent, weight):
    steps, depth, kd = weight.shape
    rows = tokens.shape[0]
    whole = pl.BlockSpec((rows, kd), lambda i: (0, 0))
    columns = pl.BlockSpec((rows, depth), lambda i: (0, i))
    return pl.pallas_call(
        products_kernel,
        grid=(steps,),
        in_specs=[columns, whole, pl.BlockSpec((1, depth, kd), lambda i: (i, 0, 0))],
        out_specs=[whole, columns],
        scratch_shapes=[pltpu.VMEM((rows, kd), jnp.float32)],
        out_shape=[
            jax.ShapeDtypeStruct((rows, kd), jnp.bfloat16),
            jax.ShapeDtypeStruct(tokens.shape, jnp.bfloat16),
        ],
        compiler_params=pltpu.CompilerParams(vmem_limit_bytes=12 * 1024 * 1024),
    )(tokens, cotangent, weight)


def bound_kernel(tok, cot, power, total):
    step = pl.program_id(0)

    @pl.when(step == 0)
    def _():
        total[...] = jnp.zeros_like(total)

    reach = jnp.max(jnp.abs(tok[...]).astype(jnp.float32), axis=1, keepdims=True)
    terms = reach * jnp.abs(cot[...]).astype(jnp.float32)
    total[...] += jnp.sum(terms.reshape(-1, NOTE, terms.shape[1]), axis=0)

    @pl.when(step == pl.num_programs(0) - 1)
    def _():
        top = jnp.maximum(jnp.sum(total[...], axis=0, keepdims=True), 2.0**-100)
        power[...] = jnp.broadcast_to(jnp.ceil(jnp.log2(top)), power.shape)


def bound_of(tokens, cotangent):
    rows, width = tokens.shape
    kd = cotangent.shape[1]
    block = min(rows, 128)
    return pl.pallas_call(
        bound_kernel,
        grid=(rows // block,),
        in_specs=[
            pl.BlockSpec((block, width), lambda i: (i, 0)),
            pl.BlockSpec((block, kd), lambda i: (i, 0)),
        ],
        out_specs=pl.BlockSpec((NOTE, kd), lambda i: (0, 0)),
        scratch_shapes=[pltpu.VMEM((NOTE, kd), jnp.float32)],
        out_shape=jax.ShapeDtypeStruct((NOTE, kd), jnp.float32),
        compiler_params=pltpu.CompilerParams(vmem_limit_bytes=60 * 1024 * 1024),
        cost_estimate=pl.CostEstimate(
            flops=2 * rows * width, bytes_accessed=2 * rows * (width + kd), transcendentals=0
        ),
    )(tokens, cotangent)


def on_device(tokens, key_weight, cotangent):
    wide, node = lax.axis_size("wide"), lax.axis_size("node")
    w_me, n_me = lax.axis_index("wide"), lax.axis_index("node")
    rows, kd = key_weight.shape
    n = wide // 2
    nz = node // n
    core, y_me = w_me & 1, w_me >> 1
    x_me, z_me = n_me % n, n_me // n
    size = {"core": 2, "first": n, "second": n, "z": nz}
    place = {
        "core": core,
        "first": jnp.where(core == 0, x_me, y_me),
        "second": jnp.where(core == 0, y_me, x_me),
        "z": z_me,
    }

    def swap(value, name, j):
        over_x, over_y = 1, 2 * node
        mask = {
            "core": (node, node),
            "first": (over_x, over_y),
            "second": (over_y, over_x),
            "z": (n, n),
        }[name]
        pairs = [(i, i ^ (j * mask[i // node % 2])) for i in range(wide * node)]
        return lax.ppermute(value, AXES, pairs)

    def pick(value, *places):
        start, extent = [0] * value.ndim, list(value.shape)
        for axis, index, *more in places:
            start[axis], extent[axis] = index, (more[0] if more else 1)
        return lax.dynamic_slice(value, start, extent)

    def in_order(value, others, name):
        out = jnp.zeros((size[name],) + value.shape, value.dtype)
        for j, part in enumerate([value, *others]):
            out = lax.dynamic_update_index_in_dim(out, part, place[name] ^ j, 0)
        return out

    def noted(value, power):
        note = jnp.broadcast_to(power, (NOTE, kd)).astype(value.dtype)
        return jnp.concatenate([value.reshape(-1, kd), note])

    def read(got, shape):
        return got[:-NOTE].reshape(shape), got[-NOTE:][:1].astype(jnp.float32)

    def gathered(value, name, power):
        message = noted(value, power)
        got = [read(swap(message, name, j), value.shape) for j in range(1, size[name])]
        return in_order(value, [one for one, _ in got], name), [other for _, other in got]

    def scale(power):
        return jnp.exp2(power)

    def factors(power, others):
        top = power
        for other in others:
            top = jnp.maximum(top, other)
        top = top + len(others).bit_length()
        return top, [scale(one - top) for one in [power, *others]]

    def given(value, name, axis, *places):
        me = place[name]
        return [swap(pick(value, (axis, me ^ j), *places), name, j) for j in range(1, size[name])]

    def taken(value, got, name, axis, factor, *places):
        total = pick(value, (axis, place[name]), *places).astype(jnp.float32) * factor[0]
        for one, other in zip(got, factor[1:]):
            total = total + one.astype(jnp.float32) * other
        return total.astype(jnp.float16)

    held = lax.optimization_barrier

    shards = [swap(key_weight, "z", j) for j in range(1, nz)]

    power, shards[0] = held((bound_of(tokens, cotangent), shards[0]))
    power = jnp.maximum(power, swap(power, "core", 1))[:1] + 1.0
    part = lax.dot_general(
        tokens, cotangent, (((0,), (0,)), ((), ())), preferred_element_type=jnp.float32
    )
    part = (part * scale(TOP - power)).astype(jnp.float16).reshape(nz, n * n, 2, rows, kd)
    others = [swap(pick(part, (0, z), (2, 1 - core)), "core", 1) for z in range(nz)]
    part, shards = held((part, shards))
    blocks = in_order(key_weight, shards, "z")

    def pair_sum(z, other):
        total = pick(part, (0, z), (2, core)).astype(jnp.float32) + other.astype(jnp.float32)
        total = total.astype(jnp.float16).reshape(n, n, rows, kd)
        return jnp.where(core == 0, total, total.transpose(1, 0, 2, 3))

    part = jnp.stack([pair_sum(z, other) for z, other in enumerate(others)])

    given_first = given(part, "first", 1)
    blocks, power_first = gathered(blocks, "first", power)
    by_first = factors(power, power_first)
    part, given_first, blocks, by_first = held((part, given_first, blocks, by_first))
    sums = taken(part, given_first, "first", 1, by_first[1])
    blocks, power_second = gathered(blocks, "second", by_first[0])
    by_second = factors(by_first[0], power_second)
    sums = taken(sums, given(sums, "second", 2), "second", 2, by_second[1])
    sums = sums.reshape(nz, rows, kd)

    other = swap(blocks, "core", 1)
    x_first = jnp.where(core == 0, blocks, other).transpose(2, 1, 0, 3, 4)
    y_first = jnp.where(core == 0, other, blocks).transpose(2, 0, 1, 3, 4)
    weight = jnp.stack([x_first, y_first], axis=3).reshape(nz, n * n * 2 * rows, kd)

    top = by_second[0]
    got = [swap(noted(pick(sums, (0, z_me ^ j)), top), "z", j) for j in range(1, nz)]
    keys, input_grad = products(tokens, cotangent, weight)
    keys, input_grad, got = held((keys, input_grad, got))
    total = pick(sums, (0, z_me))[0].astype(jnp.float32) * scale(top - TOP)
    for one, other in [read(one, (rows, kd)) for one in got]:
        total = total + one.astype(jnp.float32) * scale(other - TOP)
    total_tokens = tokens.shape[0] * wide * node
    weight_grad = total * (1.0 / jnp.sqrt(jnp.float32(total_tokens)))
    return (keys, input_grad, weight_grad)


def solution(mesh):
    placed = (P(AXES, None), P(("node", "wide"), None), P(AXES, None))
    return jax.shard_map(
        on_device,
        mesh=mesh,
        in_specs=placed,
        out_specs=(P(AXES, None), P(AXES, None), P(("node", "wide"), None)),
        check_vma=False,
    )
```

```python
import jax
import jax.numpy as jnp
from jax import lax
from jax.experimental import pallas as pl
from jax.experimental.pallas import tpu as pltpu
from jax.sharding import PartitionSpec as P

AXES = ("wide", "node")
TOP = 14.0
NOTE = 8


def products_kernel(tok, cot, weight, keys, grad, total):
    step = pl.program_id(0)

    @pl.when(step == 0)
    def _():
        total[...] = jnp.zeros_like(total)

    total[...] += jnp.dot(tok[...], weight[0], preferred_element_type=jnp.float32)
    grad[...] = lax.dot_general(
        cot[...], weight[0], (((1,), (1,)), ((), ())), preferred_element_type=jnp.float32
    ).astype(grad.dtype)

    @pl.when(step == pl.num_programs(0) - 1)
    def _():
        keys[...] = total[...].astype(keys.dtype)


def products(tokens, cotangent, weight):
    steps, depth, kd = weight.shape
    rows = tokens.shape[0]
    whole = pl.BlockSpec((rows, kd), lambda i: (0, 0))
    columns = pl.BlockSpec((rows, depth), lambda i: (0, i))
    return pl.pallas_call(
        products_kernel,
        grid=(steps,),
        in_specs=[columns, whole, pl.BlockSpec((1, depth, kd), lambda i: (i, 0, 0))],
        out_specs=[whole, columns],
        scratch_shapes=[pltpu.VMEM((rows, kd), jnp.float32)],
        out_shape=[
            jax.ShapeDtypeStruct((rows, kd), jnp.bfloat16),
            jax.ShapeDtypeStruct(tokens.shape, jnp.bfloat16),
        ],
        compiler_params=pltpu.CompilerParams(vmem_limit_bytes=12 * 1024 * 1024),
    )(tokens, cotangent, weight)


def bound_kernel(tok, cot, power, total):
    step = pl.program_id(0)

    @pl.when(step == 0)
    def _():
        total[...] = jnp.zeros_like(total)

    reach = jnp.max(jnp.abs(tok[...]).astype(jnp.float32), axis=1, keepdims=True)
    terms = reach * jnp.abs(cot[...]).astype(jnp.float32)
    total[...] += jnp.sum(terms.reshape(-1, NOTE, terms.shape[1]), axis=0)

    @pl.when(step == pl.num_programs(0) - 1)
    def _():
        top = jnp.maximum(jnp.sum(total[...], axis=0, keepdims=True), 2.0**-100)
        power[...] = jnp.broadcast_to(jnp.ceil(jnp.log2(top)), power.shape)


def bound_of(tokens, cotangent):
    rows, width = tokens.shape
    kd = cotangent.shape[1]
    block = min(rows, 256)
    return pl.pallas_call(
        bound_kernel,
        grid=(rows // block,),
        in_specs=[
            pl.BlockSpec((block, width), lambda i: (i, 0)),
            pl.BlockSpec((block, kd), lambda i: (i, 0)),
        ],
        out_specs=pl.BlockSpec((NOTE, kd), lambda i: (0, 0)),
        scratch_shapes=[pltpu.VMEM((NOTE, kd), jnp.float32)],
        out_shape=jax.ShapeDtypeStruct((NOTE, kd), jnp.float32),
        compiler_params=pltpu.CompilerParams(vmem_limit_bytes=60 * 1024 * 1024),
        cost_estimate=pl.CostEstimate(
            flops=2 * rows * width, bytes_accessed=2 * rows * (width + kd), transcendentals=0
        ),
    )(tokens, cotangent)


def on_device(tokens, key_weight, cotangent):
    wide, node = lax.axis_size("wide"), lax.axis_size("node")
    w_me, n_me = lax.axis_index("wide"), lax.axis_index("node")
    rows, kd = key_weight.shape
    half = rows // 2
    ny, nx, nz = wide // 2, 2, node // 2
    core, y_me = w_me & 1, w_me >> 1
    x_me, z_me = n_me & 1, n_me >> 1

    size = {"core": 2, "y": ny, "x": nx, "z": nz}
    place = {"core": core, "y": y_me, "x": x_me, "z": z_me}
    mask = {"core": node, "y": 2 * node, "x": 1, "z": 2}

    def swap(value, name, j):
        return lax.ppermute(value, AXES, [(i, i ^ (j * mask[name])) for i in range(wide * node)])

    def pick(value, *places):
        start, extent = [0] * value.ndim, list(value.shape)
        for axis, index, *more in places:
            start[axis], extent[axis] = index, (more[0] if more else 1)
        return lax.dynamic_slice(value, start, extent)

    def in_order(value, others, name):
        out = jnp.zeros((size[name],) + value.shape, value.dtype)
        for j, part in enumerate([value, *others]):
            out = lax.dynamic_update_index_in_dim(out, part, place[name] ^ j, 0)
        return out

    def noted(value, power):
        note = jnp.broadcast_to(power, (NOTE, kd)).astype(value.dtype)
        return jnp.concatenate([value.reshape(-1, kd), note])

    def read(got, shape):
        return got[:-NOTE].reshape(shape), got[-NOTE:][:1].astype(jnp.float32)

    def gathered(value, name, power):
        message = noted(value, power)
        got = [read(swap(message, name, j), value.shape) for j in range(1, size[name])]
        return in_order(value, [one for one, _ in got], name), [other for _, other in got]

    def scale(power):
        return jnp.exp2(power)

    def factors(power, others):
        top = power
        for other in others:
            top = jnp.maximum(top, other)
        top = top + len(others).bit_length()
        return top, [scale(one - top) for one in [power, *others]]

    def given(value, name, axis, *places):
        me = place[name]
        return [swap(pick(value, (axis, me ^ j), *places), name, j) for j in range(1, size[name])]

    def given_noted(value, name, axis, power):
        me = place[name]
        shape = value.shape[:axis] + (1,) + value.shape[axis + 1 :]
        got = [
            read(swap(noted(pick(value, (axis, me ^ j)), power), name, j), shape)
            for j in range(1, size[name])
        ]
        return [one for one, _ in got], [other for _, other in got]

    def taken(value, got, name, axis, factor, *places):
        total = pick(value, (axis, place[name]), *places).astype(jnp.float32) * factor[0]
        for one, other in zip(got, factor[1:]):
            total = total + one.astype(jnp.float32) * other
        return total.astype(jnp.float16)

    held = lax.optimization_barrier

    shards = [swap(key_weight, "z", j) for j in range(1, nz)]

    early = nz // 2
    power, shards[:early] = held((bound_of(tokens, cotangent), shards[:early]))
    power = jnp.maximum(power, swap(power, "core", 1))[:1] + 1.0
    part = lax.dot_general(
        tokens, cotangent, (((0,), (0,)), ((), ())), preferred_element_type=jnp.float32
    )
    part = (part * scale(TOP - power)).astype(jnp.float16).reshape(nz * nx * ny, 2, rows, kd)
    sent, shards[early:] = held((pick(part, (1, 1 - core)), shards[early:]))
    other = swap(sent, "core", 1)
    part, shards = held((part, shards))
    blocks = in_order(key_weight, shards, "z").reshape(nz, 2, half, kd)
    part = pick(part, (1, core)).astype(jnp.float32) + other.astype(jnp.float32)
    part = part.astype(jnp.float16).reshape(nz, nx, ny, rows, kd)

    upper, lower = (3, 0, half), (3, half, half)
    got_one, got_two = given(part, "x", 1, upper), given(part, "y", 2, lower)
    one, power_x = gathered(blocks[:, 0], "x", power)
    two, power_y = gathered(blocks[:, 1], "y", power)
    by_x, by_y = factors(power, power_x), factors(power, power_y)
    part, got_one, got_two, one, two, by_x, by_y = held(
        (part, got_one, got_two, one, two, by_x, by_y)
    )
    sum_one = taken(part, got_one, "x", 1, by_x[1], upper)
    sum_two = taken(part, got_two, "y", 2, by_y[1], lower)
    got_one, power_xy = given_noted(sum_one, "y", 2, by_x[0])
    got_two, power_yx = given_noted(sum_two, "x", 1, by_y[0])
    one = in_order(one, [swap(one, "y", j) for j in range(1, ny)], "y")
    two = in_order(two, [swap(two, "x", j) for j in range(1, nx)], "x")
    by_xy, by_yx = factors(by_x[0], power_xy), factors(by_y[0], power_yx)
    top_one = by_xy[0]
    sum_one = taken(sum_one, got_one, "y", 2, by_xy[1])
    sum_two = taken(sum_two, got_two, "x", 1, by_yx[1])
    total = jnp.concatenate([sum_one, sum_two], axis=3).reshape(nz, rows, kd)
    got = [
        swap(noted(pick(total, (0, z_me ^ j)), top_one), "z", j)
        for j in range(1, nz)
    ]
    total, one, two, got[:early] = held((total, one, two, got[:early]))
    both = jnp.stack([one.transpose(2, 1, 0, 3, 4), two.transpose(2, 0, 1, 3, 4)], axis=3)
    weight = in_order(both, [swap(both, "core", 1)], "core")
    weight = weight.transpose(1, 2, 3, 0, 4, 5, 6).reshape(nz, nx * ny * 2 * rows, kd)
    keys, input_grad = products(tokens, cotangent, weight)
    keys, input_grad, got = held((keys, input_grad, got))
    got = [read(one, (rows, kd)) for one in got]
    total = pick(total, (0, z_me))[0].astype(jnp.float32) * scale(top_one - TOP)
    for one, other in got:
        total = total + one.astype(jnp.float32) * scale(other - TOP)
    total_tokens = tokens.shape[0] * wide * node
    weight_grad = total * (1.0 / jnp.sqrt(jnp.float32(total_tokens)))
    return (keys, input_grad, weight_grad)


def solution(mesh):
    placed = (P(AXES, None), P(("node", "wide"), None), P(AXES, None))
    return jax.shard_map(
        on_device,
        mesh=mesh,
        in_specs=placed,
        out_specs=(P(AXES, None), P(AXES, None), P(("node", "wide"), None)),
        check_vma=False,
    )
```

```python
import jax
import jax.numpy as jnp
from jax import lax
from jax.experimental import pallas as pl
from jax.experimental.pallas import tpu as pltpu
from jax.sharding import PartitionSpec as P

AXES = ("wide", "node")
TOP = 14.0
NOTE = 8


def products_kernel(tok, cot, weight, keys, grad, total):
    step = pl.program_id(0)

    @pl.when(step == 0)
    def _():
        total[...] = jnp.zeros_like(total)

    total[...] += jnp.dot(tok[...], weight[0], preferred_element_type=jnp.float32)
    grad[...] = lax.dot_general(
        cot[...], weight[0], (((1,), (1,)), ((), ())), preferred_element_type=jnp.float32
    ).astype(grad.dtype)

    @pl.when(step == pl.num_programs(0) - 1)
    def _():
        keys[...] = total[...].astype(keys.dtype)


def products(tokens, cotangent, weight):
    steps, depth, kd = weight.shape
    rows = tokens.shape[0]
    whole = pl.BlockSpec((rows, kd), lambda i: (0, 0))
    columns = pl.BlockSpec((rows, depth), lambda i: (0, i))
    return pl.pallas_call(
        products_kernel,
        grid=(steps,),
        in_specs=[columns, whole, pl.BlockSpec((1, depth, kd), lambda i: (i, 0, 0))],
        out_specs=[whole, columns],
        scratch_shapes=[pltpu.VMEM((rows, kd), jnp.float32)],
        out_shape=[
            jax.ShapeDtypeStruct((rows, kd), jnp.bfloat16),
            jax.ShapeDtypeStruct(tokens.shape, jnp.bfloat16),
        ],
        compiler_params=pltpu.CompilerParams(vmem_limit_bytes=12 * 1024 * 1024),
    )(tokens, cotangent, weight)


def bound_kernel(tok, cot, power, scale, total):
    step = pl.program_id(0)

    @pl.when(step == 0)
    def _():
        total[...] = jnp.zeros_like(total)

    reach = jnp.max(jnp.abs(tok[...]).astype(jnp.float32), axis=1, keepdims=True)
    terms = reach * jnp.abs(cot[...]).astype(jnp.float32)
    total[...] += jnp.sum(terms.reshape(-1, NOTE, terms.shape[1]), axis=0)

    @pl.when(step == pl.num_programs(0) - 1)
    def _():
        top = jnp.maximum(jnp.sum(total[...], axis=0, keepdims=True), 2.0**-100)
        least = jnp.ceil(jnp.log2(top))
        power[...] = jnp.broadcast_to(least, power.shape)
        scale[...] = jnp.exp2(TOP - least)


def bound_of(tokens, cotangent):
    rows, width = tokens.shape
    kd = cotangent.shape[1]
    block = min(rows, 256)
    return pl.pallas_call(
        bound_kernel,
        grid=(rows // block,),
        in_specs=[
            pl.BlockSpec((block, width), lambda i: (i, 0)),
            pl.BlockSpec((block, kd), lambda i: (i, 0)),
        ],
        out_specs=[pl.BlockSpec((size, kd), lambda i: (0, 0)) for size in (NOTE, 1)],
        scratch_shapes=[pltpu.VMEM((NOTE, kd), jnp.float32)],
        out_shape=[jax.ShapeDtypeStruct((size, kd), jnp.float32) for size in (NOTE, 1)],
        compiler_params=pltpu.CompilerParams(vmem_limit_bytes=60 * 1024 * 1024),
        cost_estimate=pl.CostEstimate(
            flops=2 * rows * width, bytes_accessed=2 * rows * (width + kd), transcendentals=0
        ),
    )(tokens, cotangent)


def on_device(tokens, key_weight, cotangent):
    wide, node = lax.axis_size("wide"), lax.axis_size("node")
    w_me, n_me = lax.axis_index("wide"), lax.axis_index("node")
    rows, kd = key_weight.shape
    half = rows // 2
    ny, nx, nz = wide // 2, 2, node // 2
    core, y_me = w_me & 1, w_me >> 1
    x_me, z_me = n_me & 1, n_me >> 1

    size = {"core": 2, "y": ny, "x": nx, "z": nz}
    place = {"core": core, "y": y_me, "x": x_me, "z": z_me}
    mask = {"core": node, "y": 2 * node, "x": 1, "z": 2}

    def swap(value, name, j):
        return lax.ppermute(value, AXES, [(i, i ^ (j * mask[name])) for i in range(wide * node)])

    def pick(value, *places):
        start, extent = [0] * value.ndim, list(value.shape)
        for axis, index, *more in places:
            start[axis], extent[axis] = index, (more[0] if more else 1)
        return lax.dynamic_slice(value, start, extent)

    def in_order(value, others, name):
        out = jnp.zeros((size[name],) + value.shape, value.dtype)
        for j, part in enumerate([value, *others]):
            out = lax.dynamic_update_index_in_dim(out, part, place[name] ^ j, 0)
        return out

    def noted(value, power):
        note = jnp.broadcast_to(power, (NOTE, kd)).astype(value.dtype)
        return jnp.concatenate([value.reshape(-1, kd), note])

    def read(got, shape):
        return got[:-NOTE].reshape(shape), got[-NOTE:][:1].astype(jnp.float32)

    def gathered(value, name, power):
        message = noted(value, power)
        got = [read(swap(message, name, j), value.shape) for j in range(1, size[name])]
        return in_order(value, [one for one, _ in got], name), [other for _, other in got]

    def scale(power):
        return jnp.exp2(power)

    def factors(power, others):
        top = power
        for other in others:
            top = jnp.maximum(top, other)
        top = top + len(others).bit_length()
        return top, [scale(one - top) for one in [power, *others]]

    def sums(value, name, axis, factor, *places):
        me = place[name]
        got = [swap(pick(value, (axis, me ^ j), *places), name, j) for j in range(1, size[name])]
        total = pick(value, (axis, me), *places).astype(jnp.float32) * factor[0]
        for one, other in zip(got, factor[1:]):
            total = total + one.astype(jnp.float32) * other
        return total.astype(jnp.float16)

    shards = [swap(key_weight, "z", j) for j in range(1, nz)]

    power, to_top = bound_of(tokens, cotangent)
    power, shards[0] = lax.optimization_barrier((power, shards[0]))
    power, by_core = factors(power[:1], [swap(power, "core", 1)[:1]])
    part = lax.dot_general(
        tokens, cotangent, (((0,), (0,)), ((), ())), preferred_element_type=jnp.float32
    )
    part = (part * to_top).astype(jnp.float16).reshape(nz * nx * ny, 2, rows, kd)
    other = swap(pick(part, (1, 1 - core)), "core", 1)
    part, shards = lax.optimization_barrier((part, shards))
    shards = in_order(key_weight, shards, "z")
    part = pick(part, (1, core)).astype(jnp.float32) * by_core[0]
    part = part + other.astype(jnp.float32) * by_core[1]
    part = part.astype(jnp.float16).reshape(nz, nx, ny, rows, kd)

    blocks = shards.reshape(nz, 2, half, kd)
    one, power_x = gathered(blocks[:, 0], "x", power)
    two, power_y = gathered(blocks[:, 1], "y", power)
    by_x, by_y = factors(power, power_x), factors(power, power_y)
    part, one, two, by_x, by_y = lax.optimization_barrier((part, one, two, by_x, by_y))
    sum_one = sums(part, "x", 1, by_x[1], (3, 0, half))
    sum_two = sums(part, "y", 2, by_y[1], (3, half, half))
    one, power_xy = gathered(one, "y", by_x[0])
    two, power_yx = gathered(two, "x", by_y[0])
    by_xy, by_yx = factors(by_x[0], power_xy), factors(by_y[0], power_yx)
    top_one = by_xy[0]
    sum_one = sums(sum_one, "y", 2, by_xy[1])
    sum_two = sums(sum_two, "x", 1, by_yx[1])
    both = jnp.stack([one.transpose(2, 1, 0, 3, 4), two.transpose(2, 0, 1, 3, 4)], axis=3)
    weight = in_order(both, [swap(both, "core", 1)], "core")
    weight = weight.transpose(1, 2, 3, 0, 4, 5, 6).reshape(nz, nx * ny * 2 * rows, kd)

    total = jnp.concatenate([sum_one, sum_two], axis=3).reshape(nz, rows, kd)
    got = [
        swap(noted(pick(total, (0, z_me ^ j)), top_one), "z", j)
        for j in range(1, nz)
    ]
    keys, input_grad = products(tokens, cotangent, weight)
    keys, input_grad, got = lax.optimization_barrier((keys, input_grad, got))
    got = [read(one, (rows, kd)) for one in got]
    total = pick(total, (0, z_me))[0].astype(jnp.float32) * scale(top_one - TOP)
    for one, other in got:
        total = total + one.astype(jnp.float32) * scale(other - TOP)
    total_tokens = tokens.shape[0] * wide * node
    weight_grad = total * (1.0 / jnp.sqrt(jnp.float32(total_tokens)))
    return (keys, input_grad, weight_grad)


def solution(mesh):
    placed = (P(AXES, None), P(("node", "wide"), None), P(AXES, None))
    return jax.shard_map(
        on_device,
        mesh=mesh,
        in_specs=placed,
        out_specs=(P(AXES, None), P(AXES, None), P(("node", "wide"), None)),
        check_vma=False,
    )
```

```python
import jax
import jax.numpy as jnp
from jax import lax
from jax.experimental import pallas as pl
from jax.experimental.pallas import tpu as pltpu
from jax.sharding import PartitionSpec as P

AXES = ("wide", "node")
TOP = 14.0
NOTE = 8


def products_kernel(tok, cot, weight, keys, grad, total):
    step = pl.program_id(0)

    @pl.when(step == 0)
    def _():
        total[...] = jnp.zeros_like(total)

    total[...] += jnp.dot(tok[...], weight[0], preferred_element_type=jnp.float32)
    grad[...] = lax.dot_general(
        cot[...], weight[0], (((1,), (1,)), ((), ())), preferred_element_type=jnp.float32
    ).astype(grad.dtype)

    @pl.when(step == pl.num_programs(0) - 1)
    def _():
        keys[...] = total[...].astype(keys.dtype)


def products(tokens, cotangent, weight):
    steps, depth, kd = weight.shape
    rows = tokens.shape[0]
    whole = pl.BlockSpec((rows, kd), lambda i: (0, 0))
    columns = pl.BlockSpec((rows, depth), lambda i: (0, i))
    return pl.pallas_call(
        products_kernel,
        grid=(steps,),
        in_specs=[columns, whole, pl.BlockSpec((1, depth, kd), lambda i: (i, 0, 0))],
        out_specs=[whole, columns],
        scratch_shapes=[pltpu.VMEM((rows, kd), jnp.float32)],
        out_shape=[
            jax.ShapeDtypeStruct((rows, kd), jnp.bfloat16),
            jax.ShapeDtypeStruct(tokens.shape, jnp.bfloat16),
        ],
        compiler_params=pltpu.CompilerParams(vmem_limit_bytes=12 * 1024 * 1024),
    )(tokens, cotangent, weight)


def bound_kernel(tok, cot, power, scale, total):
    step = pl.program_id(0)

    @pl.when(step == 0)
    def _():
        total[...] = jnp.zeros_like(total)

    reach = jnp.max(jnp.abs(tok[...]).astype(jnp.float32), axis=1, keepdims=True)
    terms = reach * jnp.abs(cot[...]).astype(jnp.float32)
    total[...] += jnp.sum(terms.reshape(-1, NOTE, terms.shape[1]), axis=0)

    @pl.when(step == pl.num_programs(0) - 1)
    def _():
        top = jnp.maximum(jnp.sum(total[...], axis=0, keepdims=True), 2.0**-100)
        least = jnp.ceil(jnp.log2(top))
        power[...] = jnp.broadcast_to(least, power.shape)
        scale[...] = jnp.exp2(TOP - least)


def bound_of(tokens, cotangent):
    rows, width = tokens.shape
    kd = cotangent.shape[1]
    block = min(rows, 256)
    return pl.pallas_call(
        bound_kernel,
        grid=(rows // block,),
        in_specs=[
            pl.BlockSpec((block, width), lambda i: (i, 0)),
            pl.BlockSpec((block, kd), lambda i: (i, 0)),
        ],
        out_specs=[pl.BlockSpec((size, kd), lambda i: (0, 0)) for size in (NOTE, 1)],
        scratch_shapes=[pltpu.VMEM((NOTE, kd), jnp.float32)],
        out_shape=[jax.ShapeDtypeStruct((size, kd), jnp.float32) for size in (NOTE, 1)],
        compiler_params=pltpu.CompilerParams(vmem_limit_bytes=60 * 1024 * 1024),
        cost_estimate=pl.CostEstimate(
            flops=2 * rows * width, bytes_accessed=2 * rows * (width + kd), transcendentals=0
        ),
    )(tokens, cotangent)


def on_device(tokens, key_weight, cotangent):
    wide, node = lax.axis_size("wide"), lax.axis_size("node")
    w_me, n_me = lax.axis_index("wide"), lax.axis_index("node")
    rows, kd = key_weight.shape
    half = rows // 2
    ny, nx, nz = wide // 2, 2, node // 2
    core, y_me = w_me & 1, w_me >> 1
    x_me, z_me = n_me & 1, n_me >> 1

    size = {"core": 2, "y": ny, "x": nx, "z": nz}
    place = {"core": core, "y": y_me, "x": x_me, "z": z_me}
    mask = {"core": node, "y": 2 * node, "x": 1, "z": 2}

    def swap(value, name, j):
        return lax.ppermute(value, AXES, [(i, i ^ (j * mask[name])) for i in range(wide * node)])

    def pick(value, *places):
        start, extent = [0] * value.ndim, list(value.shape)
        for axis, index, *more in places:
            start[axis], extent[axis] = index, (more[0] if more else 1)
        return lax.dynamic_slice(value, start, extent)

    def in_order(value, others, name):
        out = jnp.zeros((size[name],) + value.shape, value.dtype)
        for j, part in enumerate([value, *others]):
            out = lax.dynamic_update_index_in_dim(out, part, place[name] ^ j, 0)
        return out

    def noted(value, power):
        note = jnp.broadcast_to(power, (NOTE, kd)).astype(value.dtype)
        return jnp.concatenate([value.reshape(-1, kd), note])

    def read(got, shape):
        return got[:-NOTE].reshape(shape), got[-NOTE:][:1].astype(jnp.float32)

    def gathered(value, name, power):
        message = noted(value, power)
        got = [read(swap(message, name, j), value.shape) for j in range(1, size[name])]
        return in_order(value, [one for one, _ in got], name), [other for _, other in got]

    def scale(power):
        return jnp.exp2(power)

    def factors(power, others):
        top = power
        for other in others:
            top = jnp.maximum(top, other)
        top = top + len(others).bit_length()
        return top, [scale(one - top) for one in [power, *others]]

    def sums(value, name, axis, factor, *places):
        me = place[name]
        got = [swap(pick(value, (axis, me ^ j), *places), name, j) for j in range(1, size[name])]
        total = pick(value, (axis, me), *places).astype(jnp.float32) * factor[0]
        for one, other in zip(got, factor[1:]):
            total = total + one.astype(jnp.float32) * other
        return total.astype(jnp.float16)

    shards = [swap(key_weight, "z", j) for j in range(1, nz)]

    power, to_top = bound_of(tokens, cotangent)
    power, to_top, shards[0] = lax.optimization_barrier((power, to_top, shards[0]))
    power_core = swap(power, "core", 1)
    part = lax.dot_general(
        tokens, cotangent, (((0,), (0,)), ((), ())), preferred_element_type=jnp.float32
    )
    part = (part * to_top).astype(jnp.float16).reshape(nz * nx * ny, 2, rows, kd)
    sent, power_core = lax.optimization_barrier((pick(part, (1, 1 - core)), power_core))
    other = swap(sent, "core", 1)
    power, by_core = factors(power[:1], [power_core[:1]])
    part, shards = lax.optimization_barrier((part, shards))
    shards = in_order(key_weight, shards, "z")
    part = pick(part, (1, core)).astype(jnp.float32) * by_core[0]
    part = part + other.astype(jnp.float32) * by_core[1]
    part = part.astype(jnp.float16).reshape(nz, nx, ny, rows, kd)

    blocks = shards.reshape(nz, 2, half, kd)
    one, power_x = gathered(blocks[:, 0], "x", power)
    two, power_y = gathered(blocks[:, 1], "y", power)
    by_x, by_y = factors(power, power_x), factors(power, power_y)
    part, one, two, by_x, by_y = lax.optimization_barrier((part, one, two, by_x, by_y))
    sum_one = sums(part, "x", 1, by_x[1], (3, 0, half))
    sum_two = sums(part, "y", 2, by_y[1], (3, half, half))
    one, power_xy = gathered(one, "y", by_x[0])
    two, power_yx = gathered(two, "x", by_y[0])
    by_xy, by_yx = factors(by_x[0], power_xy), factors(by_y[0], power_yx)
    top_one = by_xy[0]
    sum_one = sums(sum_one, "y", 2, by_xy[1])
    sum_two = sums(sum_two, "x", 1, by_yx[1])
    both = jnp.stack([one.transpose(2, 1, 0, 3, 4), two.transpose(2, 0, 1, 3, 4)], axis=3)
    weight = in_order(both, [swap(both, "core", 1)], "core")
    weight = weight.transpose(1, 2, 3, 0, 4, 5, 6).reshape(nz, nx * ny * 2 * rows, kd)

    total = jnp.concatenate([sum_one, sum_two], axis=3).reshape(nz, rows, kd)
    got = [
        swap(noted(pick(total, (0, z_me ^ j)), top_one), "z", j)
        for j in range(1, nz)
    ]
    keys, input_grad = products(tokens, cotangent, weight)
    keys, input_grad, got = lax.optimization_barrier((keys, input_grad, got))
    got = [read(one, (rows, kd)) for one in got]
    total = pick(total, (0, z_me))[0].astype(jnp.float32) * scale(top_one - TOP)
    for one, other in got:
        total = total + one.astype(jnp.float32) * scale(other - TOP)
    total_tokens = tokens.shape[0] * wide * node
    weight_grad = total * (1.0 / jnp.sqrt(jnp.float32(total_tokens)))
    return (keys, input_grad, weight_grad)


def solution(mesh):
    placed = (P(AXES, None), P(("node", "wide"), None), P(AXES, None))
    return jax.shard_map(
        on_device,
        mesh=mesh,
        in_specs=placed,
        out_specs=(P(AXES, None), P(AXES, None), P(("node", "wide"), None)),
        check_vma=False,
    )
```

```python
import jax
import jax.numpy as jnp
from jax import lax
from jax.experimental import pallas as pl
from jax.experimental.pallas import tpu as pltpu
from jax.sharding import PartitionSpec as P

AXES = ("wide", "node")
TOP = 14.0
NOTE = 8


def products_kernel(tok, cot, weight, keys, grad, total):
    step = pl.program_id(0)

    @pl.when(step == 0)
    def _():
        total[...] = jnp.zeros_like(total)

    total[...] += jnp.dot(tok[...], weight[0], preferred_element_type=jnp.float32)
    grad[...] = lax.dot_general(
        cot[...], weight[0], (((1,), (1,)), ((), ())), preferred_element_type=jnp.float32
    ).astype(grad.dtype)

    @pl.when(step == pl.num_programs(0) - 1)
    def _():
        keys[...] = total[...].astype(keys.dtype)


def products(tokens, cotangent, weight):
    steps, depth, kd = weight.shape
    rows = tokens.shape[0]
    whole = pl.BlockSpec((rows, kd), lambda i: (0, 0))
    columns = pl.BlockSpec((rows, depth), lambda i: (0, i))
    return pl.pallas_call(
        products_kernel,
        grid=(steps,),
        in_specs=[columns, whole, pl.BlockSpec((1, depth, kd), lambda i: (i, 0, 0))],
        out_specs=[whole, columns],
        scratch_shapes=[pltpu.VMEM((rows, kd), jnp.float32)],
        out_shape=[
            jax.ShapeDtypeStruct((rows, kd), jnp.bfloat16),
            jax.ShapeDtypeStruct(tokens.shape, jnp.bfloat16),
        ],
        compiler_params=pltpu.CompilerParams(vmem_limit_bytes=12 * 1024 * 1024),
    )(tokens, cotangent, weight)


def bound_kernel(tok, cot, power, total):
    step = pl.program_id(0)

    @pl.when(step == 0)
    def _():
        total[...] = jnp.zeros_like(total)

    reach = jnp.max(jnp.abs(tok[...]).astype(jnp.float32), axis=1, keepdims=True)
    terms = reach * jnp.abs(cot[...]).astype(jnp.float32)
    total[...] += jnp.sum(terms.reshape(-1, NOTE, terms.shape[1]), axis=0)

    @pl.when(step == pl.num_programs(0) - 1)
    def _():
        top = jnp.maximum(jnp.sum(total[...], axis=0, keepdims=True), 2.0**-100)
        power[...] = jnp.broadcast_to(jnp.ceil(jnp.log2(top)), power.shape)


def bound_of(tokens, cotangent):
    rows, width = tokens.shape
    kd = cotangent.shape[1]
    block = min(rows, 256)
    return pl.pallas_call(
        bound_kernel,
        grid=(rows // block,),
        in_specs=[
            pl.BlockSpec((block, width), lambda i: (i, 0)),
            pl.BlockSpec((block, kd), lambda i: (i, 0)),
        ],
        out_specs=pl.BlockSpec((NOTE, kd), lambda i: (0, 0)),
        scratch_shapes=[pltpu.VMEM((NOTE, kd), jnp.float32)],
        out_shape=jax.ShapeDtypeStruct((NOTE, kd), jnp.float32),
        compiler_params=pltpu.CompilerParams(vmem_limit_bytes=60 * 1024 * 1024),
        cost_estimate=pl.CostEstimate(
            flops=2 * rows * width, bytes_accessed=2 * rows * (width + kd), transcendentals=0
        ),
    )(tokens, cotangent)


def on_device(tokens, key_weight, cotangent):
    wide, node = lax.axis_size("wide"), lax.axis_size("node")
    w_me, n_me = lax.axis_index("wide"), lax.axis_index("node")
    rows, kd = key_weight.shape
    half = rows // 2
    ny, nx, nz = wide // 2, 2, node // 2
    core, y_me = w_me & 1, w_me >> 1
    x_me, z_me = n_me & 1, n_me >> 1

    size = {"core": 2, "y": ny, "x": nx, "z": nz}
    place = {"core": core, "y": y_me, "x": x_me, "z": z_me}
    mask = {"core": node, "y": 2 * node, "x": 1, "z": 2}

    def swap(value, name, j):
        return lax.ppermute(value, AXES, [(i, i ^ (j * mask[name])) for i in range(wide * node)])

    def pick(value, *places):
        start, extent = [0] * value.ndim, list(value.shape)
        for axis, index, *more in places:
            start[axis], extent[axis] = index, (more[0] if more else 1)
        return lax.dynamic_slice(value, start, extent)

    def in_order(value, others, name):
        out = jnp.zeros((size[name],) + value.shape, value.dtype)
        for j, part in enumerate([value, *others]):
            out = lax.dynamic_update_index_in_dim(out, part, place[name] ^ j, 0)
        return out

    def noted(value, power):
        note = jnp.broadcast_to(power, (NOTE, kd)).astype(value.dtype)
        return jnp.concatenate([value.reshape(-1, kd), note])

    def read(got, shape):
        return got[:-NOTE].reshape(shape), got[-NOTE:][:1].astype(jnp.float32)

    def gathered(value, name, power):
        message = noted(value, power)
        got = [read(swap(message, name, j), value.shape) for j in range(1, size[name])]
        return in_order(value, [one for one, _ in got], name), [other for _, other in got]

    def scale(power):
        return jnp.exp2(power)

    def factors(power, others):
        top = power
        for other in others:
            top = jnp.maximum(top, other)
        top = top + len(others).bit_length()
        return top, [scale(one - top) for one in [power, *others]]

    def sums(value, name, axis, factor, *places, sent=None):
        me = place[name]
        if sent is None:
            sent = [pick(value, (axis, me ^ j), *places) for j in range(1, size[name])]
        got = [swap(one, name, j) for j, one in enumerate(sent, 1)]
        total = pick(value, (axis, me), *places).astype(jnp.float32) * factor[0]
        for one, other in zip(got, factor[1:]):
            total = total + one.astype(jnp.float32) * other
        return total.astype(jnp.float16)

    shards = [swap(key_weight, "z", j) for j in range(1, nz)]

    power, shards[0] = lax.optimization_barrier((bound_of(tokens, cotangent), shards[0]))
    power = jnp.maximum(power, swap(power, "core", 1))[:1] + 1.0
    part = lax.dot_general(
        tokens, cotangent, (((0,), (0,)), ((), ())), preferred_element_type=jnp.float32
    )
    part = (part * scale(TOP - power)).astype(jnp.float16).reshape(nz * nx * ny, 2, rows, kd)
    other = swap(pick(part, (1, 1 - core)), "core", 1)
    part, shards = lax.optimization_barrier((part, shards))
    shards = in_order(key_weight, shards, "z")
    part = pick(part, (1, core)).astype(jnp.float32) + other.astype(jnp.float32)
    part = part.astype(jnp.float16).reshape(nz, nx, ny, rows, kd)

    blocks = shards.reshape(nz, 2, half, kd)
    one, power_x = gathered(blocks[:, 0], "x", power)
    two, power_y = gathered(blocks[:, 1], "y", power)
    by_x, by_y = factors(power, power_x), factors(power, power_y)
    upper, lower = (3, 0, half), (3, half, half)
    to_x = [pick(part, (1, x_me ^ j), upper) for j in range(1, nx)]
    to_y = [pick(part, (2, y_me ^ j), lower) for j in range(1, ny)]
    part, to_x, to_y, one, two, by_x, by_y = lax.optimization_barrier(
        (part, to_x, to_y, one, two, by_x, by_y)
    )
    sum_one = sums(part, "x", 1, by_x[1], upper, sent=to_x)
    sum_two = sums(part, "y", 2, by_y[1], lower, sent=to_y)
    one, power_xy = gathered(one, "y", by_x[0])
    two, power_yx = gathered(two, "x", by_y[0])
    by_xy, by_yx = factors(by_x[0], power_xy), factors(by_y[0], power_yx)
    top_one = by_xy[0]
    sum_one = sums(sum_one, "y", 2, by_xy[1])
    sum_two = sums(sum_two, "x", 1, by_yx[1])
    both = jnp.stack([one.transpose(2, 1, 0, 3, 4), two.transpose(2, 0, 1, 3, 4)], axis=3)
    weight = in_order(both, [swap(both, "core", 1)], "core")
    weight = weight.transpose(1, 2, 3, 0, 4, 5, 6).reshape(nz, nx * ny * 2 * rows, kd)

    total = jnp.concatenate([sum_one, sum_two], axis=3).reshape(nz, rows, kd)
    got = [
        swap(noted(pick(total, (0, z_me ^ j)), top_one), "z", j)
        for j in range(1, nz)
    ]
    keys, input_grad = products(tokens, cotangent, weight)
    keys, input_grad, got = lax.optimization_barrier((keys, input_grad, got))
    got = [read(one, (rows, kd)) for one in got]
    total = pick(total, (0, z_me))[0].astype(jnp.float32) * scale(top_one - TOP)
    for one, other in got:
        total = total + one.astype(jnp.float32) * scale(other - TOP)
    total_tokens = tokens.shape[0] * wide * node
    weight_grad = total * (1.0 / jnp.sqrt(jnp.float32(total_tokens)))
    return (keys, input_grad, weight_grad)


def solution(mesh):
    placed = (P(AXES, None), P(("node", "wide"), None), P(AXES, None))
    return jax.shard_map(
        on_device,
        mesh=mesh,
        in_specs=placed,
        out_specs=(P(AXES, None), P(AXES, None), P(("node", "wide"), None)),
        check_vma=False,
    )
```
